32 devices in a mesh: patch: 16 (over z, x, core), tp: 2 (over y).
Axes of the slice: x: 2, y: 2, z: 4, core: 2. Of those that a mesh axis runs over, the one named last changes fastest.
Arguments:
- hidden_states: bfloat16 [2, 2048, 3072], P(None, 'patch'), may hold values from -6 to 6
- modulation: float32 [3, 2, 3072], replicated, may hold values from -4 to 4
- qkv_weight: bfloat16 [3072, 3, 3072], P(None, None, 'tp'), may hold values from -0.109375 to 0.109375
- out_weight: bfloat16 [3072, 3072], P('tp'), may hold values from -0.109375 to 0.109375
- qk_gain: float32 [2, 128], replicated, may hold values from 0.8 to 2
- stale_kv: bfloat16 [2, 2, 2048, 3072], P(None, None, 'patch', 'tp'), may hold values from -400 to 400, as said below
Outputs:
- mixed: bfloat16 [2, 2048, 3072], P(None, 'patch', 'tp')
- fresh_kv: bfloat16 [2, 2, 2048, 3072], P(None, None, 'patch', 'tp')
The draws below stay inside these ranges and needn't reach their ends.
Inputs may be any that keep to these rules, and one draw needn't show every extreme that they name: `stale_kv`: keys and values of the previous step, of every token of every clip.
All inputs are finite; a program needn't handle non-finite values.
Results may differ from the reference program's by a relative error of at most 0.012.
The reference program's roundings to bfloat16 on the way (of `normed`, `weights` and `attended`) count: a program that leaves them out, or rounds other values in their place, can miss the bound.
Values may be sent and summed in bfloat16 or wider, within the bound.
No kernel may reach another device: no remote copies, remote signals or barrier semaphores. Data moves between devices by JAX's collectives and lax.ppermute only.
A program may use at most 192 MiB of HBM per device.

```python
import jax
import jax.numpy as jnp
from jax import lax

D = 3072
HEADS = 24
HEAD = 128
CLIPS = 2
TOK_DEV = 128
SEQ = 2048
N_PATCH = 16


def draw_stale_kv(key, part):
    key = jax.random.fold_in(key, 7)
    key_base = jax.random.fold_in(key, 0)
    shape = (2, CLIPS, SEQ, D)
    result = jnp.clip(jax.random.normal(key_base, shape, jnp.float32), -4.0, 4.0)
    return result.astype(jnp.bfloat16)


def block_levels(stream_key, extent, cuts, low, top_value):
    level, own = 1.0, jax.random.fold_in(stream_key, 6)
    for axis_at, parts in cuts:
        draws = jnp.exp(jax.random.uniform(jax.random.fold_in(own, axis_at), (parts,), jnp.float32, low / len(cuts), top_value / len(cuts)))
        level = level * jnp.repeat(draws, extent[axis_at] // parts).reshape([-1 if axis == axis_at else 1 for axis in range(len(extent))])
    return level


def gaussian(stream_key, dims, scale, reach, shards=(), kind=jnp.bfloat16):
    values = scale * jax.random.normal(stream_key, dims, jnp.float32)
    if shards:
        values = values * block_levels(stream_key, dims, shards, -0.22, 0.18)
    return jnp.clip(values, -reach, reach).astype(kind)


def setup_inputs(seed: int = 0) -> dict:
    key_of = jax.random.split(jax.random.key(seed), 7)
    hidden_states = gaussian(key_of[0], (CLIPS, SEQ, D), 1.0, 6.0, ((1, 16),))
    modulation = gaussian(key_of[1], (3, CLIPS, D), 1.0, 4.0, (), jnp.float32)
    qkv_weight = gaussian(key_of[2], (D, 3, D), D ** -0.5, 0.109375, ((2, 2),))
    out_weight = gaussian(key_of[3], (D, D), D ** -0.5, 0.109375, ((0, 2),))
    qk_gain = jnp.clip(jax.random.uniform(key_of[4], (2, HEAD), jnp.float32, 0.8, 2.0), 0.8, 2.0)
    stale_kv = draw_stale_kv(jax.random.fold_in(key_of[6], 71), 0)
    return dict(hidden_states=hidden_states, modulation=modulation, qkv_weight=qkv_weight, out_weight=out_weight, qk_gain=qk_gain, stale_kv=stale_kv)


def head_norm(values_in, gain_row):
    shaped = values_in.reshape(values_in.shape[0], values_in.shape[1], HEADS, HEAD)
    square_mean = lax.optimization_barrier(jnp.mean(shaped * shaped, axis=-1, keepdims=True))
    return (shaped * lax.rsqrt(square_mean + 1e-06) * gain_row).astype(jnp.bfloat16)

def reference(hidden_states, modulation, qkv_weight, out_weight, qk_gain, stale_kv):
    inputs = hidden_states.astype(jnp.float32)
    feature_mean = lax.optimization_barrier(jnp.mean(inputs, axis=-1, keepdims=True))
    centered = inputs - feature_mean
    feature_var = lax.optimization_barrier(jnp.mean(centered * centered, axis=-1, keepdims=True))
    normed = (centered * lax.rsqrt(feature_var + 1e-06) * (1.0 + modulation[1][:, None, :]) + modulation[0][:, None, :]).astype(jnp.bfloat16)
    normed = lax.optimization_barrier(normed)
    projected = jnp.einsum('ctd,dkh->kcth', normed.astype(jnp.float32), qkv_weight.astype(jnp.float32))
    queries = head_norm(projected[0], qk_gain[0])
    keys_new = head_norm(projected[1], qk_gain[1])
    values_new = projected[2].astype(jnp.bfloat16).reshape(CLIPS, SEQ, HEADS, HEAD)
    queries, keys_new, values_new = lax.optimization_barrier((queries, keys_new, values_new))
    fresh_kv = jnp.stack([keys_new.reshape(CLIPS, SEQ, D), values_new.reshape(CLIPS, SEQ, D)])
    stale_keys = stale_kv[0].reshape(CLIPS, SEQ, HEADS, HEAD)
    stale_values = stale_kv[1].reshape(CLIPS, SEQ, HEADS, HEAD)
    inv_scale = HEAD ** (-0.5)

    def one_patch(patch_id):
        first = (patch_id * TOK_DEV).astype(jnp.int32)
        query_block = lax.dynamic_slice_in_dim(queries, first, TOK_DEV, 1)
        key_all = lax.dynamic_update_slice_in_dim(stale_keys, lax.dynamic_slice_in_dim(keys_new, first, TOK_DEV, 1), first, 1)
        value_all = lax.dynamic_update_slice_in_dim(stale_values, lax.dynamic_slice_in_dim(values_new, first, TOK_DEV, 1), first, 1)
        scores = jnp.einsum('cqhd,ckhd->chqk', query_block.astype(jnp.float32), key_all.astype(jnp.float32)) * inv_scale
        top = lax.optimization_barrier(jnp.max(scores, axis=-1, keepdims=True))
        expo = jnp.exp(scores - top)
        total = lax.optimization_barrier(jnp.sum(expo, axis=-1))
        weights = lax.optimization_barrier(expo.astype(jnp.bfloat16))
        summed = jnp.einsum('chqk,ckhd->chqd', weights.astype(jnp.float32), value_all.astype(jnp.float32))
        attended = (summed / total[..., None]).astype(jnp.bfloat16)
        return jnp.transpose(attended, (0, 2, 1, 3)).reshape(CLIPS, TOK_DEV, D)
    blocks = lax.map(one_patch, jnp.arange(N_PATCH, dtype=jnp.int32))
    attended = jnp.transpose(blocks, (1, 0, 2, 3)).reshape(CLIPS, SEQ, D)
    attended = lax.optimization_barrier(attended)
    product = jnp.dot(attended.reshape(CLIPS * SEQ, D), out_weight, preferred_element_type=jnp.float32).reshape(CLIPS, SEQ, D)
    mixed = (inputs + modulation[2][:, None, :] * product).astype(jnp.bfloat16)
    return (mixed, fresh_kv)
```

```python
import functools
import math

import jax
import jax.numpy as jnp
from jax import lax
from jax.experimental import pallas as pl
from jax.experimental.pallas import tpu as pltpu
from jax.sharding import PartitionSpec as P

HEAD = 128
EXTRA = 16
LOG2E = 1.4426950408889634
SCALE2 = HEAD ** (-0.5) * LOG2E
MIB = 1024 * 1024
BF = jnp.bfloat16
F32 = jnp.float32


def nt(a, b):
    return lax.dot_general(a, b, (((1,), (1,)), ((), ())), preferred_element_type=F32)


def nn(a, b):
    return lax.dot_general(a, b, (((1,), (0,)), ((), ())), preferred_element_type=F32)


def params(mib, **kw):
    return pltpu.CompilerParams(vmem_limit_bytes=mib * MIB, **kw)


def norm_heads(values, gain_row):
    parts = []
    for h in range(values.shape[1] // HEAD):
        v = values[:, h * HEAD : (h + 1) * HEAD]
        square_mean = jnp.mean(v * v, axis=-1, keepdims=True)
        parts.append((v * lax.rsqrt(square_mean + 1e-06) * gain_row).astype(BF))
    return jnp.concatenate(parts, axis=1)


def cut_kernel(groups, width, pos, stale, *rest):
    outs, sems = rest[:groups], rest[groups]
    copies = []
    for s in range(groups):
        first = pl.multiple_of(lax.rem(pos[0] + s, groups) * width, HEAD)
        copies.append(
            pltpu.make_async_copy(stale.at[:, :, :, pl.ds(first, width)], outs[s], sems.at[s])
        )
    for c in copies:
        c.start()
    for c in copies:
        c.wait()


def cut_stale(pos, stale, groups):
    kv, clips, rows, cols = stale.shape
    width = cols // groups
    shape = jax.ShapeDtypeStruct((kv, clips, rows, width), BF)
    return pl.pallas_call(
        functools.partial(cut_kernel, groups, width),
        out_shape=[shape] * groups,
        in_specs=[pl.BlockSpec(memory_space=pltpu.SMEM), pl.BlockSpec(memory_space=pl.ANY)],
        out_specs=[pl.BlockSpec(memory_space=pl.ANY)] * groups,
        scratch_shapes=[pltpu.SemaphoreType.DMA((groups,))],
        compiler_params=params(8),
        name="cut_stale",
    )(pos, stale)


def query_kernel(groups, per_step, pos, hidden, mod, gain, weight, normed, whole, *slots):
    clips, rows, width_all = hidden.shape
    step = pl.program_id(0)

    @pl.when(step == 0)
    def _():
        chunk = 32
        for c in range(clips):
            for r in range(0, rows, chunk):
                x = hidden[c, r : r + chunk, :].astype(F32)
                centered = x - jnp.mean(x, axis=-1, keepdims=True)
                var = jnp.mean(centered * centered, axis=-1, keepdims=True)
                y = centered * lax.rsqrt(var + 1e-06) * (1.0 + mod[1, c : c + 1, :])
                normed[c, r : r + chunk, :] = (y + mod[0, c : c + 1, :]).astype(BF)

    x = normed[...].reshape(clips * rows, width_all)
    q = norm_heads(nn(x, weight[0]), gain[0:1, :])
    whole[...] = q.reshape(clips, rows, -1)
    width = q.shape[1] // per_step
    for j in range(per_step):
        part = q[:, j * width : (j + 1) * width].reshape(clips, rows, width)
        slot = lax.rem(step * per_step + j - pos[0] + groups, groups)
        for s in range(groups):

            @pl.when(slot == s)
            def _(s=s, part=part):
                slots[s][...] = part


def make_queries(pos, hidden, mod, gain, weight, groups):
    clips, rows, width_all = hidden.shape
    cols = weight.shape[2]
    per_step = 2 if groups % 2 == 0 else 1
    steps = groups // per_step
    width = cols // groups
    full = lambda shape: pl.BlockSpec(shape, lambda i, pos: (0,) * len(shape))
    return pl.pallas_call(
        functools.partial(query_kernel, groups, per_step),
        grid_spec=pltpu.PrefetchScalarGridSpec(
            num_scalar_prefetch=1,
            grid=(steps,),
            in_specs=[
                full(hidden.shape),
                full(mod.shape),
                full(gain.shape),
                pl.BlockSpec((1, width_all, width * per_step), lambda i, pos: (0, 0, i)),
            ],
            out_specs=[
                full(hidden.shape),
                pl.BlockSpec((clips, rows, width * per_step), lambda i, pos: (0, 0, i)),
            ]
            + [full((clips, rows, width))] * groups,
        ),
        out_shape=[
            jax.ShapeDtypeStruct(hidden.shape, BF),
            jax.ShapeDtypeStruct((clips, rows, cols), BF),
        ]
        + [jax.ShapeDtypeStruct((clips, rows, width), BF)] * groups,
        compiler_params=params(32),
        cost_estimate=pl.CostEstimate(
            flops=2 * clips * rows * width_all * cols,
            bytes_accessed=2 * width_all * cols + 8 * clips * rows * width_all,
            transcendentals=0,
        ),
        name="norm_and_queries",
    )(pos, hidden, mod, gain, weight)


def fresh_kernel(normed, gain, weight, out):
    clips, rows, width_all = normed.shape
    x = normed[...].reshape(clips * rows, width_all)
    made = nn(x, weight[0])

    @pl.when(pl.program_id(0) == 0)
    def _():
        out[0] = norm_heads(made, gain[1:2, :]).reshape(clips, rows, -1)

    @pl.when(pl.program_id(0) == 1)
    def _():
        out[0] = made.astype(BF).reshape(clips, rows, -1)


def make_fresh(normed, gain, weight):
    clips, rows, width_all = normed.shape
    cols = weight.shape[2]
    block = math.gcd(cols, 768)
    return pl.pallas_call(
        fresh_kernel,
        grid=(2, cols // block),
        in_specs=[
            pl.BlockSpec(normed.shape, lambda j, i: (0, 0, 0)),
            pl.BlockSpec(gain.shape, lambda j, i: (0, 0)),
            pl.BlockSpec((1, width_all, block), lambda j, i: (j + 1, 0, i)),
        ],
        out_specs=pl.BlockSpec((1, clips, rows, block), lambda j, i: (j, 0, 0, i)),
        out_shape=jax.ShapeDtypeStruct((2, clips, rows, cols), BF),
        compiler_params=params(32),
        cost_estimate=pl.CostEstimate(
            flops=4 * clips * rows * width_all * cols,
            bytes_accessed=4 * width_all * cols,
            transcendentals=0,
        ),
        name="fresh_keys_and_values",
    )(normed, gain, weight)


def own_kernel(q, kv, acc, top, total):
    rows = q.shape[1]
    ones = jnp.ones((rows, HEAD), BF)
    for h in range(q.shape[2] // HEAD):
        at = slice(h * HEAD, (h + 1) * HEAD)
        scores = nt(q[0, :, at], kv[0, 0, :, at])
        peak = jnp.max(scores, axis=-1, keepdims=True)
        weights = jnp.exp2((scores - peak) * SCALE2).astype(BF)
        summed = nn(weights, jnp.concatenate([kv[1, 0, :, at], ones], axis=1))
        acc[0, :, at] = summed[:, :HEAD]
        total[0, :, at] = summed[:, HEAD:]
        top[0, :, at] = jnp.broadcast_to(peak * SCALE2, (rows, HEAD))


def attend_own(queries, fresh):
    clips, rows, cols = queries.shape
    wide = jax.ShapeDtypeStruct(queries.shape, F32)
    block = pl.BlockSpec((1, rows, cols), lambda c: (c, 0, 0))
    return pl.pallas_call(
        own_kernel,
        grid=(clips,),
        in_specs=[block, pl.BlockSpec((2, 1, rows, cols), lambda c: (0, c, 0, 0))],
        out_specs=[block] * 3,
        out_shape=[wide] * 3,
        compiler_params=params(24),
        cost_estimate=pl.CostEstimate(
            flops=4 * clips * rows * rows * cols,
            bytes_accessed=18 * clips * rows * cols,
            transcendentals=clips * rows * rows * cols // HEAD,
        ),
        name="attend_own",
    )(queries, fresh)


def group_kernel(shifts, inner, blocks, first, last, *refs):
    refs = list(refs)
    queries = [refs.pop(0) for _ in range(blocks)]
    cached = [[refs.pop(0) for _ in range(inner)] for _ in shifts]
    state = None if first else (refs.pop(0), refs.pop(0))
    outs = refs
    rows, width = queries[0].shape[1:]
    ones = jnp.ones((inner * rows, HEAD), BF)
    for h in range(width // HEAD):
        at = slice(h * HEAD, (h + 1) * HEAD)
        keys = [jnp.concatenate([r[0, 0, :, at] for r in g], axis=0) for g in cached]
        values = [
            jnp.concatenate([jnp.concatenate([r[1, 0, :, at] for r in g], axis=0), ones], axis=1)
            for g in cached
        ]
        for b in range(blocks):
            q = queries[b][0, :, at]
            scores = []
            for s, k in zip(shifts, keys):
                sc = nt(q, k)
                if s == b:
                    sc = jnp.concatenate(
                        [jnp.full((rows, rows), -1e30, F32), sc[:, rows:]], axis=1
                    )
                scores.append(sc)
            peak = functools.reduce(
                jnp.maximum, [jnp.max(sc, axis=-1, keepdims=True) for sc in scores]
            )
            if not first:
                before = state[0][0, h, b]
                peak = jnp.maximum(before, peak)
            peak = jnp.broadcast_to(peak, (rows, HEAD))
            wide = jnp.concatenate([peak] * inner, axis=1)
            summed = None
            for sc, v in zip(scores, values):
                part = nn(jnp.exp2((sc - wide) * SCALE2).astype(BF), v)
                summed = part if summed is None else summed + part
            if not first:
                keep = jnp.exp2((before - peak) * SCALE2)
                summed = summed + state[1][0, h, b] * jnp.concatenate([keep, keep], axis=1)
            if last:
                total = summed[:, HEAD:]
                outs[b][0, 0:rows, at] = (summed[:, :HEAD] / total).astype(BF)
                level = jnp.transpose(peak * SCALE2 + jnp.log2(total))[0:8, :]
                high = level.astype(BF)
                mid = (level - high.astype(F32)).astype(BF)
                low = (level - high.astype(F32) - mid.astype(F32)).astype(BF)
                row = lax.broadcasted_iota(jnp.int32, (8, HEAD), 0)
                three = jnp.where(
                    row == 0,
                    high.astype(F32),
                    jnp.where(row == 1, mid.astype(F32), low.astype(F32)),
                )
                outs[b][0, rows : rows + EXTRA, at] = jnp.concatenate([three, three], axis=0).astype(BF)
            else:
                outs[0][0, h, b] = peak
                outs[1][0, h, b] = summed


def attend_groups(queries, cached, shifts, state, last):
    blocks = len(queries)
    clips, rows, width = queries[0].shape
    heads = width // HEAD
    inner = len(cached[0])
    first = state is None
    q_spec = pl.BlockSpec((1, rows, width), lambda c: (c, 0, 0))
    kv_spec = pl.BlockSpec((2, 1, rows, width), lambda c: (0, c, 0, 0))
    top_spec = pl.BlockSpec((1, heads, blocks, rows, HEAD), lambda c: (c, 0, 0, 0, 0))
    sum_spec = pl.BlockSpec((1, heads, blocks, rows, 2 * HEAD), lambda c: (c, 0, 0, 0, 0))
    flat = [a for g in cached for a in g]
    args = list(queries) + flat + ([] if first else list(state))
    if last:
        out_specs = [pl.BlockSpec((1, rows + EXTRA, width), lambda c: (c, 0, 0))] * blocks
        out_shape = [jax.ShapeDtypeStruct((clips, rows + EXTRA, width), BF)] * blocks
    else:
        out_specs = [top_spec, sum_spec]
        out_shape = [
            jax.ShapeDtypeStruct((clips, heads, blocks, rows, HEAD), F32),
            jax.ShapeDtypeStruct((clips, heads, blocks, rows, 2 * HEAD), F32),
        ]
    pairs = clips * heads * blocks * rows * len(flat) * rows
    return pl.pallas_call(
        functools.partial(group_kernel, tuple(shifts), inner, blocks, first, last),
        grid=(clips,),
        in_specs=[q_spec] * blocks
        + [kv_spec] * len(flat)
        + ([] if first else [top_spec, sum_spec]),
        out_specs=out_specs,
        out_shape=out_shape,
        compiler_params=params(40),
        cost_estimate=pl.CostEstimate(
            flops=6 * pairs * HEAD,
            bytes_accessed=4 * clips * rows * width * len(flat),
            transcendentals=pairs,
        ),
        name="attend_groups",
    )(*args)


def out_kernel(groups, pos, *refs):
    back = refs[:groups]
    acc, top, total, weight, send, keep, product = refs[groups:]
    step = pl.program_id(0)
    clips, rows, width = acc.shape

    for s in range(groups):

        @pl.when(step == s)
        def _(s=s):
            parts = []
            for c in range(clips):
                cols = []
                for h in range(width // HEAD):
                    at = slice(h * HEAD, (h + 1) * HEAD)
                    three = back[s][c, rows : rows + 8, at].astype(F32)
                    level = three[0:1, :] + three[1:2, :] + three[2:3, :]
                    level = jnp.transpose(jnp.broadcast_to(level, (rows, HEAD)))
                    own = top[c, :, at]
                    peak = jnp.maximum(level, own)
                    w_own, w_back = jnp.exp2(own - peak), jnp.exp2(level - peak)
                    mixed = acc[c, :, at] * w_own + back[s][c, 0:rows, at].astype(F32) * w_back
                    cols.append((mixed / (total[c, :, at] * w_own + w_back)).astype(BF))
                parts.append(jnp.concatenate(cols, axis=1))
            part = nn(jnp.concatenate(parts, axis=0), weight[...])
            if s == 0:
                product[...] = part
            else:
                product[...] += part

    @pl.when(step == groups - 1)
    def _():
        half = product.shape[1] // 2
        mine = pl.multiple_of(pos[1] * half, HEAD)
        other = pl.multiple_of((1 - pos[1]) * half, HEAD)
        send[...] = product[:, pl.ds(other, half)].astype(BF).reshape(send.shape)
        keep[...] = product[:, pl.ds(mine, half)].reshape(keep.shape)


def project_out(pos, back, acc, top, total, weight):
    groups = len(back)
    clips, rows, width_all = acc.shape
    width = width_all // groups
    cols = weight.shape[1]
    full = lambda shape: pl.BlockSpec(shape, lambda i, pos: (0,) * len(shape))
    own = pl.BlockSpec((clips, rows, width), lambda i, pos: (0, 0, lax.rem(pos[0] + i, groups)))
    half = (clips, rows, cols // 2)
    return pl.pallas_call(
        functools.partial(out_kernel, groups),
        grid_spec=pltpu.PrefetchScalarGridSpec(
            num_scalar_prefetch=1,
            grid=(groups,),
            in_specs=[full(back[0].shape)] * groups
            + [own] * 3
            + [pl.BlockSpec((width, cols), lambda i, pos: (lax.rem(pos[0] + i, groups), 0))],
            out_specs=[full(half), full(half)],
            scratch_shapes=[pltpu.VMEM((clips * rows, cols), F32)],
        ),
        out_shape=[jax.ShapeDtypeStruct(half, BF), jax.ShapeDtypeStruct(half, F32)],
        compiler_params=params(32),
        cost_estimate=pl.CostEstimate(
            flops=2 * clips * rows * width_all * cols,
            bytes_accessed=2 * width_all * cols,
            transcendentals=2 * clips * rows * width_all,
        ),
        name="merge_and_project",
    )(pos, *back, acc, top, total, weight)


def final_kernel(pos, hidden, mod, keep, got, out):
    for c in range(hidden.shape[0]):
        total = keep[c] + got[c].astype(F32)
        out[c] = (hidden[c].astype(F32) + mod[2, c : c + 1, :] * total).astype(BF)


def finish(pos, hidden, mod, keep, got):
    full = lambda shape: pl.BlockSpec(shape, lambda i, pos: (0,) * len(shape))
    half = keep.shape
    return pl.pallas_call(
        final_kernel,
        grid_spec=pltpu.PrefetchScalarGridSpec(
            num_scalar_prefetch=1,
            grid=(1,),
            in_specs=[
                pl.BlockSpec(half, lambda i, pos: (0, 0, pos[1])),
                pl.BlockSpec(mod.shape[:2] + half[2:], lambda i, pos: (0, 0, pos[1])),
                full(half),
                full(half),
            ],
            out_specs=full(half),
        ),
        out_shape=jax.ShapeDtypeStruct(half, BF),
        compiler_params=params(24),
        name="gate_and_add",
    )(pos, hidden, mod, keep, got)


def spread_heads(groups, hidden_states, modulation, qkv_weight, out_weight, qk_gain, stale_kv):
    patches = lax.axis_size("patch")
    inner = patches // groups
    plane = lax.axis_index("patch") // inner
    pos = jnp.stack([plane, lax.axis_index("tp")]).astype(jnp.int32)

    def along(value, shift):
        pairs = [(i, (i + inner * shift) % patches) for i in range(patches)]
        return lax.ppermute(value, "patch", pairs)

    def across(value, bit):
        return lax.ppermute(value, "patch", [(i, i ^ bit) for i in range(patches)])

    weights = jnp.transpose(qkv_weight, (1, 0, 2))
    cut = cut_stale(pos, stale_kv, groups)
    order = [1, 3, 2] if groups == 4 else list(range(1, groups))
    held = {0: [cut[0]]}
    for s in order:
        held[s] = [along(cut[s], s)]
    bit = inner // 2
    while bit:
        for s in held:
            held[s] = held[s] + [across(v, bit) for v in held[s]]
        bit //= 2
    normed, queries, *slots = make_queries(pos, hidden_states, modulation, qk_gain, weights, groups)
    asked = [slots[0]] + [along(slots[s], s) for s in range(1, groups)]
    fresh_kv = make_fresh(normed, qk_gain, weights)
    acc, top, total = attend_own(queries, fresh_kv)

    calls = [[0, 1, 3], [2]] if groups == 4 else [[s] for s in range(groups)]
    state = None
    for at, shifts in enumerate(calls):
        state = attend_groups(asked, [held[s] for s in shifts], shifts, state, at == len(calls) - 1)
    back = [state[0]] + [along(state[s], -s) for s in range(1, groups)]
    send, keep = project_out(pos, back, acc, top, total, out_weight)
    got = lax.ppermute(send, "tp", [(0, 1), (1, 0)])
    mixed = finish(pos, hidden_states, modulation, keep, got)
    return mixed, fresh_kv


def head_norm(values_in, gain_row, heads_here):
    shaped = values_in.reshape(values_in.shape[0], values_in.shape[1], heads_here, HEAD)
    square_mean = jnp.mean(shaped * shaped, axis=-1, keepdims=True)
    return (shaped * lax.rsqrt(square_mean + 1e-06) * gain_row).astype(BF)


def gather_all(hidden_states, modulation, qkv_weight, out_weight, qk_gain, stale_kv):
    clip_count, row_count, width_all = hidden_states.shape
    heads_here = qkv_weight.shape[2] // HEAD
    inputs = hidden_states.astype(F32)
    feature_mean = jnp.mean(inputs, axis=-1, keepdims=True)
    centered = inputs - feature_mean
    feature_var = jnp.mean(centered * centered, axis=-1, keepdims=True)
    normed = (
        centered * lax.rsqrt(feature_var + 1e-06) * (1.0 + modulation[1][:, None, :])
        + modulation[0][:, None, :]
    ).astype(BF)
    projected = jnp.einsum("ctd,dkh->kcth", normed, qkv_weight, preferred_element_type=F32)
    queries = head_norm(projected[0], qk_gain[0], heads_here)
    keys_new = head_norm(projected[1], qk_gain[1], heads_here)
    values_new = projected[2].astype(BF).reshape(clip_count, row_count, heads_here, HEAD)
    fresh_kv = jnp.stack(
        [keys_new.reshape(clip_count, row_count, -1), values_new.reshape(clip_count, row_count, -1)]
    )
    own_first = lax.axis_index("patch") * row_count
    gathered = lax.all_gather(stale_kv, "patch", axis=2, tiled=True)
    gathered = lax.dynamic_update_slice_in_dim(gathered, fresh_kv, own_first, 2)
    count = gathered.shape[2]
    tile_keys = gathered[0].reshape(clip_count, count, heads_here, HEAD)
    tile_values = gathered[1].reshape(clip_count, count, heads_here, HEAD)
    scores = jnp.einsum("cqhd,ckhd->chqk", queries, tile_keys, preferred_element_type=F32)
    scores = scores * HEAD ** (-0.5)
    expo = jnp.exp(scores - jnp.max(scores, axis=-1, keepdims=True))
    summed = jnp.einsum(
        "chqk,ckhd->chqd", expo.astype(BF), tile_values, preferred_element_type=F32
    )
    attended = (summed / jnp.sum(expo, axis=-1)[..., None]).astype(BF)
    attended = jnp.transpose(attended, (0, 2, 1, 3)).reshape(clip_count, row_count, -1)
    product = jnp.einsum("cth,hd->ctd", attended, out_weight, preferred_element_type=F32)
    col_count = width_all // lax.axis_size("tp")
    col_first = lax.axis_index("tp") * col_count
    summed_part = lax.psum_scatter(
        product.astype(BF), "tp", scatter_dimension=2, tiled=True
    ).astype(F32)
    input_part = lax.dynamic_slice_in_dim(inputs, col_first, col_count, 2)
    gate_part = lax.dynamic_slice_in_dim(modulation[2], col_first, col_count, 1)
    mixed = (input_part + gate_part[:, None, :] * summed_part).astype(BF)
    return (mixed, fresh_kv)


def per_device(*arrays):
    heads_here = arrays[2].shape[2] // HEAD
    patches = lax.axis_size("patch")
    groups = math.gcd(heads_here, patches)
    inner = patches // groups
    if groups > 1 and inner & (inner - 1) == 0 and lax.axis_size("tp") == 2:
        return spread_heads(groups, *arrays)
    return gather_all(*arrays)


def solution(mesh):
    in_specs = (
        P(None, "patch", None),
        P(),
        P(None, None, "tp"),
        P("tp", None),
        P(),
        P(None, None, "patch", "tp"),
    )
    out_specs = (P(None, "patch", "tp"), P(None, None, "patch", "tp"))
    return jax.shard_map(
        per_device, mesh=mesh, in_specs=in_specs, out_specs=out_specs, check_vma=False
    )
```

```python
import functools
import math

import jax
import jax.numpy as jnp
from jax import lax
from jax.experimental import pallas as pl
from jax.experimental.pallas import tpu as pltpu
from jax.sharding import PartitionSpec as P

HEAD = 128
EXTRA = 16
LOG2E = 1.4426950408889634
SCALE2 = HEAD ** (-0.5) * LOG2E
MIB = 1024 * 1024
BF = jnp.bfloat16
F32 = jnp.float32


SMALL = pl.CostEstimate(flops=1000, bytes_accessed=1000, transcendentals=0)
LARGE = pl.CostEstimate(flops=10**10, bytes_accessed=10**8, transcendentals=0)


def nt(a, b):
    return lax.dot_general(a, b, (((1,), (1,)), ((), ())), preferred_element_type=F32)


def nn(a, b):
    return lax.dot_general(a, b, (((1,), (0,)), ((), ())), preferred_element_type=F32)


def params(mib, **kw):
    return pltpu.CompilerParams(vmem_limit_bytes=mib * MIB, **kw)


def norm_heads(values, gain_row):
    parts = []
    for h in range(values.shape[1] // HEAD):
        v = values[:, h * HEAD : (h + 1) * HEAD]
        square_mean = jnp.mean(v * v, axis=-1, keepdims=True)
        parts.append((v * lax.rsqrt(square_mean + 1e-06) * gain_row).astype(BF))
    return jnp.concatenate(parts, axis=1)


def full(shape):
    return pl.BlockSpec(shape, lambda *_: (0,) * len(shape))


def out_of(shape, dtype=BF):
    return jax.ShapeDtypeStruct(shape, dtype)


ANYWHERE = pl.BlockSpec(memory_space=pltpu.HBM)
SCALARS = pl.BlockSpec(memory_space=pltpu.SMEM)


def copy_all(sems, pairs):
    copies = [pltpu.make_async_copy(a, b, sems.at[i]) for i, (a, b) in enumerate(pairs)]
    for c in copies:
        c.start()
    for c in copies:
        c.wait()


def cut_kernel(width, pos, stale, *rest):
    outs, sems = rest[:-1], rest[-1]
    pairs = []
    for s, out in enumerate(outs):
        cols = pl.ds(pl.multiple_of((pos[0] ^ s) * width, HEAD), width)
        pairs.append((stale.at[:, :, :, cols], out))
    copy_all(sems, pairs)


def cut_stale(pos, stale, groups):
    kv, clips, rows, cols = stale.shape
    width = cols // groups
    return pl.pallas_call(
        functools.partial(cut_kernel, width),
        out_shape=[out_of((kv, clips, rows, width))] * groups,
        in_specs=[SCALARS, ANYWHERE],
        out_specs=[ANYWHERE] * groups,
        scratch_shapes=[pltpu.SemaphoreType.DMA((groups,))],
        compiler_params=params(8),
        name="cut_stale",
    )(pos, stale)


def pack_kernel(pos, *refs):
    blocks, out, sems = refs[:-2], refs[-2], refs[-1]
    copy_all(sems, [(r.at[:, 1 - pos[2]], out.at[i]) for i, r in enumerate(blocks)])


def pack(pos, *blocks):
    kv, clips, rows, width = blocks[0].shape
    return pl.pallas_call(
        pack_kernel,
        out_shape=out_of((len(blocks), kv, rows, width)),
        in_specs=[SCALARS] + [ANYWHERE] * len(blocks),
        out_specs=ANYWHERE,
        scratch_shapes=[pltpu.SemaphoreType.DMA((len(blocks),))],
        compiler_params=params(8),
        name="pack",
    )(pos, *blocks)


def query_kernel(groups, per_step, pos, hidden, got, mod, gain, weight, normed, whole, *slots):
    rows = got.shape[0]
    step = pl.program_id(0)

    @pl.when(step == 0)
    def _():
        chunk = 32
        shift, scale = mod[0, pl.ds(pos[2], 1), :], 1.0 + mod[1, pl.ds(pos[2], 1), :]
        for half in range(2):
            for r in range(0, rows, chunk):
                x = hidden[0, r : r + chunk, :] if half == 0 else got[r : r + chunk, :]
                x = x.astype(F32)
                centered = x - jnp.mean(x, axis=-1, keepdims=True)
                var = jnp.mean(centered * centered, axis=-1, keepdims=True)
                y = centered * lax.rsqrt(var + 1e-06) * scale + shift
                normed[half * rows + r : half * rows + r + chunk, :] = y.astype(BF)

    q = norm_heads(nn(normed[...], weight[0]), gain[0:1, :])
    whole[...] = q
    width = q.shape[1] // per_step
    for j in range(per_step):
        part = q[:, j * width : (j + 1) * width]
        slot = (step * per_step + j) ^ pos[0]
        for s in range(groups):

            @pl.when(slot == s)
            def _(s=s, part=part):
                if s < 2:
                    slots[s][...] = part
                else:
                    slots[2 * s - 2][...] = part[:rows]
                    slots[2 * s - 1][...] = part[rows:]


def make_queries(pos, hidden, got, mod, gain, weight, groups):
    rows, width_all = got.shape
    cols = weight.shape[2]
    per_step = 2 if groups % 2 == 0 else 1
    steps = groups // per_step
    width = cols // groups
    wide = width * per_step
    return pl.pallas_call(
        functools.partial(query_kernel, groups, per_step),
        grid_spec=pltpu.PrefetchScalarGridSpec(
            num_scalar_prefetch=1,
            grid=(steps,),
            in_specs=[
                pl.BlockSpec((1, rows, width_all), lambda i, pos: (pos[2], 0, 0)),
                full(got.shape),
                full(mod.shape),
                full(gain.shape),
                pl.BlockSpec((1, width_all, wide), lambda i, pos: (0, 0, i)),
            ],
            out_specs=[
                full((2 * rows, width_all)),
                pl.BlockSpec((2 * rows, wide), lambda i, pos: (0, i)),
            ]
            + [full((2 * rows, width))] * 2
            + [full((rows, width))] * (2 * groups - 4),
        ),
        out_shape=[out_of((2 * rows, width_all)), out_of((2 * rows, cols))]
        + [out_of((2 * rows, width))] * 2
        + [out_of((rows, width))] * (2 * groups - 4),
        compiler_params=params(32),
        cost_estimate=SMALL,
        name="norm_and_queries",
    )(pos, hidden, got, mod, gain, weight)


def fresh_kernel(slot, normed, gain, weight, *refs):
    mine, other = refs[-2:]
    rows = mine.shape[1]
    made = nn(normed[...], weight[0])
    made = norm_heads(made, gain[1:2, :]) if slot == 0 else made.astype(BF)
    mine[0] = made[:rows]
    other[0] = made[rows:]


def make_fresh(slot, normed, gain, weight, before=()):
    rows, width_all = normed.shape
    cols = weight.shape[2]
    block = math.gcd(cols, 768)
    out = pl.BlockSpec((1, rows // 2, block), lambda i: (slot, 0, i))
    return pl.pallas_call(
        functools.partial(fresh_kernel, slot),
        grid=(cols // block,),
        in_specs=[
            full(normed.shape),
            full(gain.shape),
            pl.BlockSpec((1, width_all, block), lambda i: (slot + 1, 0, i)),
        ]
        + [ANYWHERE] * len(before),
        out_specs=[out, out],
        out_shape=[out_of((2, rows // 2, cols))] * 2,
        input_output_aliases={3 + i: i for i in range(len(before))},
        compiler_params=params(32),
        cost_estimate=SMALL,
        name="fresh_keys" if slot == 0 else "fresh_values",
    )(normed, gain, weight, *before)


def place_kernel(pos, mine, got, out, sems):
    clip = pos[2]
    copy_all(sems, [(mine, out.at[:, clip]), (got, out.at[:, 1 - clip])])


def place_fresh(pos, mine, got):
    kv, rows, cols = mine.shape
    return pl.pallas_call(
        place_kernel,
        out_shape=out_of((kv, 2, rows, cols)),
        in_specs=[SCALARS, ANYWHERE, ANYWHERE],
        out_specs=ANYWHERE,
        scratch_shapes=[pltpu.SemaphoreType.DMA((2,))],
        compiler_params=params(8),
        name="place_fresh",
    )(pos, mine, got)


def own_kernel(q, mine, other, acc, top, total):
    rows = mine.shape[1]
    ones = jnp.ones((rows, HEAD), BF)
    for j, kv in enumerate((mine, other)):
        here = slice(j * rows, (j + 1) * rows)
        for h in range(q.shape[1] // HEAD):
            at = slice(h * HEAD, (h + 1) * HEAD)
            scores = nt(q[here, at], kv[0, :, at])
            peak = jnp.max(scores, axis=-1, keepdims=True)
            weights = jnp.exp2((scores - peak) * SCALE2).astype(BF)
            summed = nn(weights, jnp.concatenate([kv[1, :, at], ones], axis=1))
            acc[here, at] = summed[:, :HEAD]
            total[here, at] = summed[:, HEAD:]
            top[here, at] = jnp.broadcast_to(peak * SCALE2, (rows, HEAD))


def attend_own(queries, mine, other):
    block = math.gcd(queries.shape[1], 768)
    rows, cols = queries.shape
    wide = pl.BlockSpec((rows, block), lambda i: (0, i))
    kv = pl.BlockSpec((2, rows // 2, block), lambda i: (0, 0, i))
    return pl.pallas_call(
        own_kernel,
        grid=(cols // block,),
        in_specs=[wide, kv, kv],
        out_specs=[wide] * 3,
        out_shape=[out_of((rows, cols), F32)] * 3,
        compiler_params=params(24),
        cost_estimate=SMALL,
        name="attend_own",
    )(queries, mine, other)


def group_kernel(part, blocks, pos, *refs):
    queries = refs[:blocks]
    cached = [refs[blocks + 4 * g : blocks + 4 * g + 4] for g in range(blocks)]
    outs = refs[5 * blocks :]
    rows = queries[0].shape[0]
    ones = jnp.ones((4 * rows, HEAD), BF)
    keys = [jnp.concatenate([r[0] for r in g], axis=0) for g in cached]
    values = [jnp.concatenate([r[1] for r in g], axis=0) for g in cached]
    values = [jnp.concatenate([v, ones], axis=1) for v in values]
    for b in range(blocks):
        q = queries[b][...]
        scores = []
        for s in range(blocks):
            sc = nt(q, keys[s])
            if s == b:
                own = [sc[:, j * rows : (j + 1) * rows] for j in range(4)]
                own[part] = jnp.full((rows, rows), -1e30, F32)
                sc = jnp.concatenate(own, axis=1)
            scores.append(sc)
        peak = functools.reduce(
            jnp.maximum, [jnp.max(sc, axis=-1, keepdims=True) for sc in scores]
        )
        summed = None
        for sc, v in zip(scores, values):
            term = nn(jnp.exp2((sc - peak) * SCALE2).astype(BF), v)
            summed = term if summed is None else summed + term
        total = summed[:, HEAD:]
        outs[b][0:rows, :] = (summed[:, :HEAD] / total).astype(BF)
        level = jnp.transpose(peak * SCALE2 + jnp.log2(total))[0:8, :]
        high = level.astype(BF).astype(F32)
        mid = (level - high).astype(BF).astype(F32)
        low = level - high - mid
        row = lax.broadcasted_iota(jnp.int32, (8, HEAD), 0)
        three = jnp.where(row == 0, high, jnp.where(row == 1, mid, low))
        outs[b][rows : rows + EXTRA, :] = jnp.concatenate([three, three], axis=0).astype(BF)


def attend_groups(part, pos, queries, cached):
    blocks = len(queries)
    rows, width = queries[-1].shape
    flat = [a for g in cached for a in g]

    def spec(place):
        if place is None:
            return pl.BlockSpec((2, None, rows, HEAD), lambda h, pos: (0, pos[2], 0, h))
        return pl.BlockSpec((None, 2, rows, HEAD), lambda h, pos: (place, 0, 0, h))

    return pl.pallas_call(
        functools.partial(group_kernel, part, blocks),
        grid_spec=pltpu.PrefetchScalarGridSpec(
            num_scalar_prefetch=1,
            grid=(width // HEAD,),
            in_specs=[pl.BlockSpec((rows, HEAD), lambda h, pos: (part, h))] * 2
            + [pl.BlockSpec((rows, HEAD), lambda h, pos: (0, h))] * (blocks - 2)
            + [spec(place) for _, place in flat],
            out_specs=[pl.BlockSpec((rows + EXTRA, HEAD), lambda h, pos: (0, h))] * blocks,
        ),
        out_shape=[out_of((rows + EXTRA, width))] * blocks,
        compiler_params=params(32),
        cost_estimate=SMALL,
        name="attend_groups",
    )(pos, *queries, *[array for array, _ in flat])


def out_kernel(groups, pos, *refs):
    back = refs[:groups]
    acc, top, total, weight, send, keep, product = refs[groups:]
    step = pl.program_id(0)
    rows, width = acc.shape

    for s in range(groups):

        @pl.when(step == s)
        def _(s=s):
            cols = []
            for h in range(width // HEAD):
                at = slice(h * HEAD, (h + 1) * HEAD)
                three = back[s][rows : rows + 8, at].astype(F32)
                level = three[0:1, :] + three[1:2, :] + three[2:3, :]
                level = jnp.transpose(jnp.broadcast_to(level, (rows, HEAD)))
                own = top[:, at]
                peak = jnp.maximum(level, own)
                w_own, w_back = jnp.exp2(own - peak), jnp.exp2(level - peak)
                mixed = acc[:, at] * w_own + back[s][0:rows, at].astype(F32) * w_back
                cols.append((mixed / (total[:, at] * w_own + w_back)).astype(BF))
            part = nn(jnp.concatenate(cols, axis=1), weight[...])
            if s == 0:
                product[...] = part
            else:
                product[...] += part

    @pl.when(step == groups - 1)
    def _():
        half = product.shape[1] // 2
        mine = pl.multiple_of(pos[1] * half, HEAD)
        other = pl.multiple_of((1 - pos[1]) * half, HEAD)
        send[...] = product[:, pl.ds(other, half)].astype(BF)
        keep[...] = product[:, pl.ds(mine, half)]


def project_out(part, pos, back, acc, top, total, weight):
    groups = len(back)
    rows, width_all = acc.shape[0] // 2, acc.shape[1]
    width = width_all // groups
    cols = weight.shape[1]
    own = pl.BlockSpec((rows, width), lambda i, pos: (part, pos[0] ^ i))
    half = (rows, cols // 2)
    return pl.pallas_call(
        functools.partial(out_kernel, groups),
        grid_spec=pltpu.PrefetchScalarGridSpec(
            num_scalar_prefetch=1,
            grid=(groups,),
            in_specs=[full(back[0].shape)] * groups
            + [own] * 3
            + [pl.BlockSpec((width, cols), lambda i, pos: (pos[0] ^ i, 0))],
            out_specs=[full(half), full(half)],
            scratch_shapes=[pltpu.VMEM((rows, cols), F32)],
        ),
        out_shape=[out_of(half), out_of(half, F32)],
        compiler_params=params(24),
        cost_estimate=LARGE,
        name="merge_and_project",
    )(pos, *back, acc, top, total, weight)


def gated(pos, rows_in, mod, keep, got):
    gate = mod[2, pl.ds(pos[2], 1), :]
    return (rows_in.astype(F32) + gate * (keep[...] + got[...].astype(F32))).astype(BF)


def other_rows_kernel(pos, hidden, mod, keep, got, out):
    out[...] = gated(pos, hidden[...], mod, keep, got)


def my_rows_kernel(pos, hidden, mod, keep, got, theirs, out):
    out[pl.ds(pos[2], 1)] = gated(pos, hidden[0], mod, keep, got)[None]
    out[pl.ds(1 - pos[2], 1)] = theirs[...][None]


def finish(pos, hidden, mod, keep, got, theirs=None):
    half = keep.shape
    if theirs is None:
        hidden_spec = pl.BlockSpec(half, lambda i, pos: (0, pos[1]))
        extra, shape, body = [], half, other_rows_kernel
    else:
        hidden_spec = pl.BlockSpec((1,) + half, lambda i, pos: (pos[2], 0, pos[1]))
        extra, shape, body = [theirs], (2,) + half, my_rows_kernel
    return pl.pallas_call(
        body,
        grid_spec=pltpu.PrefetchScalarGridSpec(
            num_scalar_prefetch=1,
            grid=(1,),
            in_specs=[
                hidden_spec,
                pl.BlockSpec(mod.shape[:2] + half[1:], lambda i, pos: (0, 0, pos[1])),
            ]
            + [full(half)] * (2 + len(extra)),
            out_specs=full(shape),
        ),
        out_shape=out_of(shape),
        compiler_params=params(24),
        cost_estimate=SMALL,
        name="gate_and_add",
    )(pos, hidden, mod, keep, got, *extra)


def tie(value, *others):
    return lax.optimization_barrier((value, others))[0]


def spread_heads(groups, hidden_states, modulation, qkv_weight, out_weight, qk_gain, stale_kv):
    patches = lax.axis_size("patch")
    inner = patches // groups
    patch = lax.axis_index("patch")
    pos = jnp.stack([patch // inner, lax.axis_index("tp"), patch % 2]).astype(jnp.int32)

    def across(value, bit):
        return lax.ppermute(value, "patch", [(i, i ^ bit) for i in range(patches)])

    def along(value, step):
        return across(value, inner * step)

    weights = jnp.transpose(qkv_weight, (1, 0, 2))
    step = lax.optimization_barrier

    cut = cut_stale(pos, stale_kv, groups)
    near, one, two = cut[0], along(cut[1], 1), along(cut[2], 2)
    far_near = across(near, 2)
    hidden_now = tie(hidden_states, *cut)
    hidden_for = lax.dynamic_index_in_dim(hidden_now, 1 - pos[2], 0, keepdims=False)
    hidden_got = across(hidden_for, 1)
    normed, queries, *slots = make_queries(
        pos, hidden_states, hidden_got, modulation, qk_gain, weights, groups
    )
    fresh = make_fresh(0, normed, qk_gain, weights)
    normed, queries, slots, fresh, near, one, two, far_near, cut_three = step(
        (normed, queries, slots, fresh, near, one, two, far_near, cut[3])
    )

    three, asked_one = along(cut_three, 3), along(slots[1], 1)
    far_one, far_two = across(one, 2), across(two, 2)
    swap_a = across(pack(pos, near, far_near, one, two), 1)
    fresh = make_fresh(1, normed, qk_gain, weights, fresh)
    own = attend_own(queries, *fresh)
    three, asked_one, far_one, far_two, swap_a, own, slots = step(
        (three, asked_one, far_one, far_two, swap_a, own, slots)
    )

    far_three = across(three, 2)
    their_queries = [slots[0], asked_one] + [along(slots[2 * s - 1], s) for s in (2, 3)]
    swap_b = across(pack(pos, far_one, far_two, three), 1)
    far_three, their_queries, swap_b, slots, asked_one = step(
        (far_three, their_queries, swap_b, slots, asked_one)
    )

    my_queries = [slots[0], asked_one] + [along(slots[2 * s - 2], s) for s in (2, 3)]
    held = [
        [(near, None), (swap_a, 0), (far_near, None), (swap_a, 1)],
        [(one, None), (swap_a, 2), (far_one, None), (swap_b, 0)],
        [(two, None), (swap_a, 3), (far_two, None), (swap_b, 1)],
        [(three, None), (swap_b, 2), (far_three, None), (across(far_three, 1), None)],
    ]
    theirs = attend_groups(1, pos, their_queries, held)
    theirs, my_queries = step((theirs, my_queries))

    back = [theirs[0]] + [along(theirs[s], s) for s in range(1, groups)]
    mine = attend_groups(0, pos, my_queries, held)
    mine, back = step((mine, back))

    mine_back = [mine[0]] + [along(mine[s], s) for s in range(1, groups)]
    swap = [(0, 1), (1, 0)]
    send, keep = project_out(1, pos, back, *own, out_weight)
    got = lax.ppermute(send, "tp", swap)
    mine_back[0] = tie(mine_back[0], send)

    my_send, my_keep = project_out(0, pos, mine_back, *own, out_weight)
    my_got = lax.ppermute(my_send, "tp", swap)
    fresh_got = across(tie(fresh[1], send), 1)
    fresh_kv = place_fresh(pos, tie(fresh[0], my_send), fresh_got)
    theirs = finish(pos, hidden_got, modulation, tie(keep, my_send), got)
    mixed = finish(pos, hidden_states, modulation, my_keep, my_got, across(theirs, 1))
    return mixed, fresh_kv


def head_norm(values_in, gain_row, heads_here):
    shaped = values_in.reshape(values_in.shape[0], values_in.shape[1], heads_here, HEAD)
    square_mean = jnp.mean(shaped * shaped, axis=-1, keepdims=True)
    return (shaped * lax.rsqrt(square_mean + 1e-06) * gain_row).astype(BF)


def gather_all(hidden_states, modulation, qkv_weight, out_weight, qk_gain, stale_kv):
    clip_count, row_count, width_all = hidden_states.shape
    heads_here = qkv_weight.shape[2] // HEAD
    inputs = hidden_states.astype(F32)
    feature_mean = jnp.mean(inputs, axis=-1, keepdims=True)
    centered = inputs - feature_mean
    feature_var = jnp.mean(centered * centered, axis=-1, keepdims=True)
    normed = (
        centered * lax.rsqrt(feature_var + 1e-06) * (1.0 + modulation[1][:, None, :])
        + modulation[0][:, None, :]
    ).astype(BF)
    projected = jnp.einsum("ctd,dkh->kcth", normed, qkv_weight, preferred_element_type=F32)
    queries = head_norm(projected[0], qk_gain[0], heads_here)
    keys_new = head_norm(projected[1], qk_gain[1], heads_here)
    values_new = projected[2].astype(BF).reshape(clip_count, row_count, heads_here, HEAD)
    fresh_kv = jnp.stack(
        [keys_new.reshape(clip_count, row_count, -1), values_new.reshape(clip_count, row_count, -1)]
    )
    own_first = lax.axis_index("patch") * row_count
    gathered = lax.all_gather(stale_kv, "patch", axis=2, tiled=True)
    gathered = lax.dynamic_update_slice_in_dim(gathered, fresh_kv, own_first, 2)
    count = gathered.shape[2]
    tile_keys = gathered[0].reshape(clip_count, count, heads_here, HEAD)
    tile_values = gathered[1].reshape(clip_count, count, heads_here, HEAD)
    scores = jnp.einsum("cqhd,ckhd->chqk", queries, tile_keys, preferred_element_type=F32)
    scores = scores * HEAD ** (-0.5)
    expo = jnp.exp(scores - jnp.max(scores, axis=-1, keepdims=True))
    summed = jnp.einsum(
        "chqk,ckhd->chqd", expo.astype(BF), tile_values, preferred_element_type=F32
    )
    attended = (summed / jnp.sum(expo, axis=-1)[..., None]).astype(BF)
    attended = jnp.transpose(attended, (0, 2, 1, 3)).reshape(clip_count, row_count, -1)
    product = jnp.einsum("cth,hd->ctd", attended, out_weight, preferred_element_type=F32)
    col_count = width_all // lax.axis_size("tp")
    col_first = lax.axis_index("tp") * col_count
    summed_part = lax.psum_scatter(
        product.astype(BF), "tp", scatter_dimension=2, tiled=True
    ).astype(F32)
    input_part = lax.dynamic_slice_in_dim(inputs, col_first, col_count, 2)
    gate_part = lax.dynamic_slice_in_dim(modulation[2], col_first, col_count, 1)
    mixed = (input_part + gate_part[:, None, :] * summed_part).astype(BF)
    return (mixed, fresh_kv)


def per_device(*arrays):
    clips = arrays[0].shape[0]
    heads_here = arrays[2].shape[2] // HEAD
    patches = lax.axis_size("patch")
    groups = math.gcd(heads_here, patches)
    if clips == 2 and groups == 4 and patches == 4 * groups and lax.axis_size("tp") == 2:
        return spread_heads(groups, *arrays)
    return gather_all(*arrays)


def solution(mesh):
    in_specs = (
        P(None, "patch", None),
        P(),
        P(None, None, "tp"),
        P("tp", None),
        P(),
        P(None, None, "patch", "tp"),
    )
    out_specs = (P(None, "patch", "tp"), P(None, None, "patch", "tp"))
    return jax.shard_map(
        per_device, mesh=mesh, in_specs=in_specs, out_specs=out_specs, check_vma=False
    )
```

```python
import functools
import math

import jax
import jax.numpy as jnp
from jax import lax
from jax.experimental import pallas as pl
from jax.experimental.pallas import tpu as pltpu
from jax.sharding import PartitionSpec as P

HEAD = 128
EXTRA = 16
LOG2E = 1.4426950408889634
SCALE2 = HEAD ** (-0.5) * LOG2E
MIB = 1024 * 1024
BF = jnp.bfloat16
F32 = jnp.float32


SMALL = pl.CostEstimate(flops=1000, bytes_accessed=1000, transcendentals=0)
LARGE = pl.CostEstimate(flops=10**10, bytes_accessed=10**8, transcendentals=0)


def nt(a, b):
    return lax.dot_general(a, b, (((1,), (1,)), ((), ())), preferred_element_type=F32)


def nn(a, b):
    return lax.dot_general(a, b, (((1,), (0,)), ((), ())), preferred_element_type=F32)


def params(mib, **kw):
    return pltpu.CompilerParams(vmem_limit_bytes=mib * MIB, **kw)


def norm_heads(values, gain_row):
    parts = []
    for h in range(values.shape[1] // HEAD):
        v = values[:, h * HEAD : (h + 1) * HEAD]
        square_mean = jnp.mean(v * v, axis=-1, keepdims=True)
        parts.append((v * lax.rsqrt(square_mean + 1e-06) * gain_row).astype(BF))
    return jnp.concatenate(parts, axis=1)


def full(shape):
    return pl.BlockSpec(shape, lambda *_: (0,) * len(shape))


def out_of(shape, dtype=BF):
    return jax.ShapeDtypeStruct(shape, dtype)


ANYWHERE = pl.BlockSpec(memory_space=pltpu.HBM)
SCALARS = pl.BlockSpec(memory_space=pltpu.SMEM)
RESIDENT = pl.BlockSpec(memory_space=pltpu.VMEM)


def copy_all(sems, pairs):
    copies = [pltpu.make_async_copy(a, b, sems.at[i]) for i, (a, b) in enumerate(pairs)]
    for c in copies:
        c.start()
    for c in copies:
        c.wait()


def cut_kernel(width, pos, stale, *rest):
    outs, sems = rest[:-1], rest[-1]
    pairs = []
    for s, out in enumerate(outs):
        cols = pl.ds(pl.multiple_of((pos[0] ^ s) * width, HEAD), width)
        pairs.append((stale.at[:, :, :, cols], out))
    copy_all(sems, pairs)


def cut_stale(pos, stale, groups):
    kv, clips, rows, cols = stale.shape
    width = cols // groups
    return pl.pallas_call(
        functools.partial(cut_kernel, width),
        out_shape=[out_of((kv, clips, rows, width))] * groups,
        in_specs=[SCALARS, ANYWHERE],
        out_specs=[ANYWHERE] * groups,
        scratch_shapes=[pltpu.SemaphoreType.DMA((groups,))],
        compiler_params=params(8),
        name="cut_stale",
    )(pos, stale)


def halves_kernel(block, keys, values, sems):
    copy_all(sems, [(block.at[0], keys), (block.at[1], values)])


def halves(block):
    return pl.pallas_call(
        halves_kernel,
        out_shape=[out_of(block.shape[1:])] * 2,
        in_specs=[ANYWHERE],
        out_specs=[ANYWHERE] * 2,
        scratch_shapes=[pltpu.SemaphoreType.DMA((2,))],
        compiler_params=params(8),
        name="halves",
    )(block)


def pack_kernel(counts, pos, *refs):
    refs, out, sems = list(refs[:-2]), refs[-2], refs[-1]
    pairs, other = [], 1 - pos[2]
    for i, count in enumerate(counts):
        if count == 1:
            pairs.append((refs.pop(0).at[:, other], out.at[i]))
        else:
            pairs += [(refs.pop(0).at[other], out.at[i, kv]) for kv in range(2)]
    copy_all(sems, pairs)


def pack(pos, *blocks):
    rows, width = blocks[0][0].shape[-2:]
    flat = [a for block in blocks for a in block]
    return pl.pallas_call(
        functools.partial(pack_kernel, [len(block) for block in blocks]),
        out_shape=out_of((len(blocks), 2, rows, width)),
        in_specs=[SCALARS] + [ANYWHERE] * len(flat),
        out_specs=ANYWHERE,
        scratch_shapes=[pltpu.SemaphoreType.DMA((len(flat),))],
        compiler_params=params(8),
        name="pack",
    )(pos, *flat)


def query_kernel(groups, per_step, pos, hidden, got, mod, gain, weight, normed, whole, *slots):
    rows = got.shape[0]
    step = pl.program_id(0)

    @pl.when(step == 0)
    def _():
        chunk = 32
        shift, scale = mod[0, pl.ds(pos[2], 1), :], 1.0 + mod[1, pl.ds(pos[2], 1), :]
        for half in range(2):
            for r in range(0, rows, chunk):
                x = hidden[0, r : r + chunk, :] if half == 0 else got[r : r + chunk, :]
                x = x.astype(F32)
                centered = x - jnp.mean(x, axis=-1, keepdims=True)
                var = jnp.mean(centered * centered, axis=-1, keepdims=True)
                y = centered * lax.rsqrt(var + 1e-06) * scale + shift
                normed[half * rows + r : half * rows + r + chunk, :] = y.astype(BF)

    q = norm_heads(nn(normed[...], weight[0]), gain[0:1, :])
    whole[...] = q
    width = q.shape[1] // per_step
    for j in range(per_step):
        part = q[:, j * width : (j + 1) * width]
        slot = (step * per_step + j) ^ pos[0]
        for s in range(groups):

            @pl.when(slot == s)
            def _(s=s, part=part):
                if s < 2:
                    slots[s][...] = part
                else:
                    slots[2 * s - 2][...] = part[:rows]
                    slots[2 * s - 1][...] = part[rows:]


def make_queries(pos, hidden, got, mod, gain, weight, groups):
    rows, width_all = got.shape
    cols = weight.shape[2]
    per_step = 2 if groups % 2 == 0 else 1
    steps = groups // per_step
    width = cols // groups
    wide = width * per_step
    return pl.pallas_call(
        functools.partial(query_kernel, groups, per_step),
        grid_spec=pltpu.PrefetchScalarGridSpec(
            num_scalar_prefetch=1,
            grid=(steps,),
            in_specs=[
                pl.BlockSpec((1, rows, width_all), lambda i, pos: (pos[2], 0, 0)),
                full(got.shape),
                full(mod.shape),
                full(gain.shape),
                pl.BlockSpec((1, width_all, wide), lambda i, pos: (0, 0, i)),
            ],
            out_specs=[
                full((2 * rows, width_all)),
                pl.BlockSpec((2 * rows, wide), lambda i, pos: (0, i)),
            ]
            + [full((2 * rows, width))] * 2
            + [full((rows, width))] * (2 * groups - 4),
        ),
        out_shape=[out_of((2 * rows, width_all)), out_of((2 * rows, cols))]
        + [out_of((2 * rows, width))] * 2
        + [out_of((rows, width))] * (2 * groups - 4),
        compiler_params=params(32),
        cost_estimate=SMALL,
        name="norm_and_queries",
    )(pos, hidden, got, mod, gain, weight)


def fresh_kernel(slot, normed, gain, weight, *refs):
    mine, other = refs[-2:]
    rows = mine.shape[1]
    made = nn(normed[...], weight[0])
    made = norm_heads(made, gain[1:2, :]) if slot == 0 else made.astype(BF)
    mine[0] = made[:rows]
    other[0] = made[rows:]


def make_fresh(slot, normed, gain, weight, before=()):
    rows, width_all = normed.shape
    cols = weight.shape[2]
    block = math.gcd(cols, 768)
    out = pl.BlockSpec((1, rows // 2, block), lambda i: (slot, 0, i))
    return pl.pallas_call(
        functools.partial(fresh_kernel, slot),
        grid=(cols // block,),
        in_specs=[
            full(normed.shape),
            full(gain.shape),
            pl.BlockSpec((1, width_all, block), lambda i: (slot + 1, 0, i)),
        ]
        + [ANYWHERE] * len(before),
        out_specs=[out, out],
        out_shape=[out_of((2, rows // 2, cols))] * 2,
        input_output_aliases={3 + i: i for i in range(len(before))},
        compiler_params=params(32),
        cost_estimate=SMALL,
        name="fresh_keys" if slot == 0 else "fresh_values",
    )(normed, gain, weight, *before)


def place_kernel(pos, mine, got, out, sems):
    clip = pos[2]
    copy_all(sems, [(mine, out.at[:, clip]), (got, out.at[:, 1 - clip])])


def place_fresh(pos, mine, got):
    kv, rows, cols = mine.shape
    return pl.pallas_call(
        place_kernel,
        out_shape=out_of((kv, 2, rows, cols)),
        in_specs=[SCALARS, ANYWHERE, ANYWHERE],
        out_specs=ANYWHERE,
        scratch_shapes=[pltpu.SemaphoreType.DMA((2,))],
        compiler_params=params(8),
        name="place_fresh",
    )(pos, mine, got)


def own_kernel(q, mine, other, acc, top, total):
    rows = mine.shape[1]
    ones = jnp.ones((rows, HEAD), BF)
    for j, kv in enumerate((mine, other)):
        here = slice(j * rows, (j + 1) * rows)
        for h in range(q.shape[1] // HEAD):
            at = slice(h * HEAD, (h + 1) * HEAD)
            scores = nt(q[here, at], kv[0, :, at])
            peak = jnp.max(scores, axis=-1, keepdims=True)
            weights = jnp.exp2((scores - peak) * SCALE2).astype(BF)
            summed = nn(weights, jnp.concatenate([kv[1, :, at], ones], axis=1))
            acc[here, at] = summed[:, :HEAD]
            total[here, at] = summed[:, HEAD:]
            top[here, at] = jnp.broadcast_to(peak * SCALE2, (rows, HEAD))


def attend_own(queries, mine, other):
    block = math.gcd(queries.shape[1], 768)
    rows, cols = queries.shape
    wide = pl.BlockSpec((rows, block), lambda i: (0, i))
    kv = pl.BlockSpec((2, rows // 2, block), lambda i: (0, 0, i))
    return pl.pallas_call(
        own_kernel,
        grid=(cols // block,),
        in_specs=[wide, kv, kv],
        out_specs=[wide] * 3,
        out_shape=[out_of((rows, cols), F32)] * 3,
        compiler_params=params(24),
        cost_estimate=SMALL,
        name="attend_own",
    )(queries, mine, other)


def group_kernel(part, blocks, places, pos, *refs):
    count = sum(n for n, _ in places)
    queries, refs, outs = refs[:blocks], list(refs[blocks : blocks + count]), refs[blocks + count :]
    cached = [[refs.pop(0) for _ in range(n)] for n, _ in places]
    rows, width = queries[-1].shape
    mine = slice(part * rows, (part + 1) * rows)
    clip = pl.ds(pos[2], 1)
    ones = jnp.ones((4 * rows, HEAD), BF)

    def load(kv, group, at):
        parts = []
        for block, (n, place) in list(zip(cached, places))[4 * group : 4 * group + 4]:
            if place is not None:
                parts.append(block[0][place, kv, :, at])
            elif n == 2:
                parts.append(block[kv][clip, :, at][0])
            else:
                parts.append(block[0][kv, clip, :, at][0])
        return jnp.concatenate(parts, axis=0)

    for h in range(width // HEAD):
        at = slice(h * HEAD, (h + 1) * HEAD)
        keys = [load(0, g, at) for g in range(blocks)]
        values = [jnp.concatenate([load(1, g, at), ones], axis=1) for g in range(blocks)]
        for b in range(blocks):
            q = queries[b][mine if b < 2 else slice(None), at]
            scores = []
            for s in range(blocks):
                sc = nt(q, keys[s])
                if s == b:
                    own = [sc[:, j * rows : (j + 1) * rows] for j in range(4)]
                    own[part] = jnp.full((rows, rows), -1e30, F32)
                    sc = jnp.concatenate(own, axis=1)
                scores.append(sc)
            peak = functools.reduce(
                jnp.maximum, [jnp.max(sc, axis=-1, keepdims=True) for sc in scores]
            )
            summed = None
            for sc, v in zip(scores, values):
                term = nn(jnp.exp2((sc - peak) * SCALE2).astype(BF), v)
                summed = term if summed is None else summed + term
            total = summed[:, HEAD:]
            outs[b][0:rows, at] = (summed[:, :HEAD] / total).astype(BF)
            level = jnp.transpose(peak * SCALE2 + jnp.log2(total))[0:8, :]
            high = level.astype(BF).astype(F32)
            mid = (level - high).astype(BF).astype(F32)
            low = level - high - mid
            row = lax.broadcasted_iota(jnp.int32, (8, HEAD), 0)
            three = jnp.where(row == 0, high, jnp.where(row == 1, mid, low))
            outs[b][rows : rows + EXTRA, at] = jnp.concatenate([three, three], axis=0).astype(BF)


def attend_groups(part, pos, queries, cached):
    blocks = len(queries)
    rows, width = queries[-1].shape
    flat = [a for g in cached for a in g]
    arrays = [a for block, _ in flat for a in block]
    places = [(len(block), place) for block, place in flat]
    return pl.pallas_call(
        functools.partial(group_kernel, part, blocks, places),
        in_specs=[SCALARS] + [RESIDENT] * (blocks + len(arrays)),
        out_specs=[RESIDENT] * blocks,
        out_shape=[out_of((rows + EXTRA, width))] * blocks,
        compiler_params=params(32),
        cost_estimate=SMALL,
        name="attend_groups",
    )(pos, *queries, *arrays)


def out_kernel(part, groups, pos, *refs):
    back = refs[:groups]
    acc, top, total, weight, send, keep, attended = refs[groups:]
    rows = send.shape[0]
    width = acc.shape[1] // groups
    mine = slice(part * rows, (part + 1) * rows)
    for s in range(groups):
        for h in range(width // HEAD):
            at = slice(h * HEAD, (h + 1) * HEAD)
            cols = pl.ds(pl.multiple_of((pos[0] ^ s) * width + h * HEAD, HEAD), HEAD)
            three = back[s][rows : rows + 8, at].astype(F32)
            level = three[0:1, :] + three[1:2, :] + three[2:3, :]
            level = jnp.transpose(jnp.broadcast_to(level, (rows, HEAD)))
            own = top[mine, cols]
            peak = jnp.maximum(level, own)
            w_own, w_back = jnp.exp2(own - peak), jnp.exp2(level - peak)
            mixed = acc[mine, cols] * w_own + back[s][0:rows, at].astype(F32) * w_back
            attended[:, cols] = (mixed / (total[mine, cols] * w_own + w_back)).astype(BF)
    half = weight.shape[1] // 2
    block = math.gcd(half, 768)
    for out, place in ((send, 1 - pos[1]), (keep, pos[1])):
        for i in range(0, half, block):
            cols = pl.ds(pl.multiple_of(place * half + i, HEAD), block)
            out[:, i : i + block] = nn(attended[...], weight[:, cols]).astype(out.dtype)


def project_out(part, pos, back, acc, top, total, weight):
    groups = len(back)
    rows, width_all = acc.shape[0] // 2, acc.shape[1]
    half = (rows, weight.shape[1] // 2)
    return pl.pallas_call(
        functools.partial(out_kernel, part, groups),
        in_specs=[SCALARS] + [RESIDENT] * (groups + 4),
        out_specs=[RESIDENT] * 2,
        out_shape=[out_of(half), out_of(half, F32)],
        scratch_shapes=[pltpu.VMEM((rows, width_all), BF)],
        compiler_params=params(32),
        cost_estimate=LARGE,
        name="merge_and_project",
    )(pos, *back, acc, top, total, weight)


def gated(pos, rows_in, mod, keep, got):
    half = keep.shape[1]
    gate = mod[2, pl.ds(pos[2], 1), pl.ds(pl.multiple_of(pos[1] * half, HEAD), half)]
    return (rows_in.astype(F32) + gate * (keep[...] + got[...].astype(F32))).astype(BF)


def other_rows_kernel(pos, hidden, mod, keep, got, out):
    half = keep.shape[1]
    cols = pl.ds(pl.multiple_of(pos[1] * half, HEAD), half)
    out[...] = gated(pos, hidden[:, cols], mod, keep, got)


def my_rows_kernel(pos, hidden, mod, keep, got, theirs, out):
    half = keep.shape[1]
    cols = pl.ds(pl.multiple_of(pos[1] * half, HEAD), half)
    mine, other = pl.ds(pos[2], 1), pl.ds(1 - pos[2], 1)
    out[mine] = gated(pos, hidden[mine, :, cols][0], mod, keep, got)[None]
    out[other] = theirs[...][None]


def finish(pos, hidden, mod, keep, got, *theirs):
    shape = (2,) * len(theirs) + keep.shape
    return pl.pallas_call(
        my_rows_kernel if theirs else other_rows_kernel,
        in_specs=[SCALARS] + [RESIDENT] * (4 + len(theirs)),
        out_specs=RESIDENT,
        out_shape=out_of(shape),
        compiler_params=params(24),
        cost_estimate=SMALL,
        name="gate_and_add",
    )(pos, hidden, mod, keep, got, *theirs)


def tie(value, *others):
    return lax.optimization_barrier((value, others))[0]


def spread_heads(groups, hidden_states, modulation, qkv_weight, out_weight, qk_gain, stale_kv):
    patches = lax.axis_size("patch")
    inner = patches // groups
    patch = lax.axis_index("patch")
    pos = jnp.stack([patch // inner, lax.axis_index("tp"), patch % 2]).astype(jnp.int32)

    def across(value, bit):
        return lax.ppermute(value, "patch", [(i, i ^ bit) for i in range(patches)])

    def along(value, step):
        return across(value, inner * step)

    weights = jnp.transpose(qkv_weight, (1, 0, 2))
    step = lax.optimization_barrier

    cut = cut_stale(pos, stale_kv, groups)
    near, two, one = cut[:1], [along(cut[2], 2)], [along(cut[1], 1)]
    far_near = [across(near[0], 2)]
    hidden_now = tie(hidden_states, *cut)
    hidden_for = lax.dynamic_index_in_dim(hidden_now, 1 - pos[2], 0, keepdims=False)
    hidden_got = across(hidden_for, 1)
    normed, queries, *slots = make_queries(
        pos, hidden_states, hidden_got, modulation, qk_gain, weights, groups
    )
    normed, queries, slots, near, one, far_near, cut_three = step(
        (normed, queries, slots, near, one, far_near, cut[3])
    )

    three = [along(cut_three, 3)]
    far_one = [across(a, 2) for a in halves(one[0])]
    fresh = make_fresh(0, normed, qk_gain, weights)
    two, far_one, fresh, slots, queries, normed = step(
        (two, far_one, fresh, slots, queries, normed)
    )

    far_two = [across(a, 2) for a in halves(two[0])]
    asked = [slots[0], along(slots[1], 1)]
    fresh = make_fresh(1, normed, qk_gain, weights, fresh)
    three, far_two, asked, fresh, slots, queries = step(
        (three, far_two, asked, fresh, slots, queries)
    )

    far_three = [across(three[0], 2)]
    their_far = [along(slots[2 * s - 1], s) for s in (2, 3)]
    swapped = [across(pack(pos, near, far_near, one, far_one, two, far_two, three), 1)]
    own = attend_own(queries, *fresh)
    far_three, their_far, asked, swapped, own, slots = step(
        (far_three, their_far, asked, swapped, own, slots)
    )

    my_far = [along(slots[2 * s - 2], s) for s in (2, 3)]
    their_queries, my_queries = asked + their_far, asked + my_far
    held = [
        [(near, None), (swapped, 0), (far_near, None), (swapped, 1)],
        [(one, None), (swapped, 2), (far_one, None), (swapped, 3)],
        [(two, None), (swapped, 4), (far_two, None), (swapped, 5)],
        [(three, None), (swapped, 6), (far_three, None), ([across(far_three[0], 1)], None)],
    ]
    theirs = attend_groups(1, pos, their_queries, held)
    theirs, my_queries = step((theirs, my_queries))
    back = [theirs[0]] + [along(theirs[s], s) for s in range(1, groups)]
    my_queries[0] = tie(my_queries[0], theirs)
    mine = attend_groups(0, pos, my_queries, held)
    mine_back = [mine[0]] + [along(mine[s], s) for s in range(1, groups)]
    back[0] = tie(back[0], mine)
    swap = [(0, 1), (1, 0)]
    send, keep = project_out(1, pos, back, *own, out_weight)
    got = lax.ppermute(send, "tp", swap)
    mine_back[0] = tie(mine_back[0], send)

    my_send, my_keep = project_out(0, pos, mine_back, *own, out_weight)
    my_got = lax.ppermute(my_send, "tp", swap)
    fresh_got = across(tie(fresh[1], send), 1)
    fresh_kv = place_fresh(pos, tie(fresh[0], my_send), fresh_got)
    theirs = finish(pos, hidden_got, modulation, tie(keep, my_send), got)
    mixed = finish(pos, hidden_states, modulation, my_keep, my_got, across(theirs, 1))
    return mixed, fresh_kv


def head_norm(values_in, gain_row, heads_here):
    shaped = values_in.reshape(values_in.shape[0], values_in.shape[1], heads_here, HEAD)
    square_mean = jnp.mean(shaped * shaped, axis=-1, keepdims=True)
    return (shaped * lax.rsqrt(square_mean + 1e-06) * gain_row).astype(BF)


def gather_all(hidden_states, modulation, qkv_weight, out_weight, qk_gain, stale_kv):
    clip_count, row_count, width_all = hidden_states.shape
    heads_here = qkv_weight.shape[2] // HEAD
    inputs = hidden_states.astype(F32)
    feature_mean = jnp.mean(inputs, axis=-1, keepdims=True)
    centered = inputs - feature_mean
    feature_var = jnp.mean(centered * centered, axis=-1, keepdims=True)
    normed = (
        centered * lax.rsqrt(feature_var + 1e-06) * (1.0 + modulation[1][:, None, :])
        + modulation[0][:, None, :]
    ).astype(BF)
    projected = jnp.einsum("ctd,dkh->kcth", normed, qkv_weight, preferred_element_type=F32)
    queries = head_norm(projected[0], qk_gain[0], heads_here)
    keys_new = head_norm(projected[1], qk_gain[1], heads_here)
    values_new = projected[2].astype(BF).reshape(clip_count, row_count, heads_here, HEAD)
    fresh_kv = jnp.stack(
        [keys_new.reshape(clip_count, row_count, -1), values_new.reshape(clip_count, row_count, -1)]
    )
    own_first = lax.axis_index("patch") * row_count
    gathered = lax.all_gather(stale_kv, "patch", axis=2, tiled=True)
    gathered = lax.dynamic_update_slice_in_dim(gathered, fresh_kv, own_first, 2)
    count = gathered.shape[2]
    tile_keys = gathered[0].reshape(clip_count, count, heads_here, HEAD)
    tile_values = gathered[1].reshape(clip_count, count, heads_here, HEAD)
    scores = jnp.einsum("cqhd,ckhd->chqk", queries, tile_keys, preferred_element_type=F32)
    scores = scores * HEAD ** (-0.5)
    expo = jnp.exp(scores - jnp.max(scores, axis=-1, keepdims=True))
    summed = jnp.einsum(
        "chqk,ckhd->chqd", expo.astype(BF), tile_values, preferred_element_type=F32
    )
    attended = (summed / jnp.sum(expo, axis=-1)[..., None]).astype(BF)
    attended = jnp.transpose(attended, (0, 2, 1, 3)).reshape(clip_count, row_count, -1)
    product = jnp.einsum("cth,hd->ctd", attended, out_weight, preferred_element_type=F32)
    col_count = width_all // lax.axis_size("tp")
    col_first = lax.axis_index("tp") * col_count
    summed_part = lax.psum_scatter(
        product.astype(BF), "tp", scatter_dimension=2, tiled=True
    ).astype(F32)
    input_part = lax.dynamic_slice_in_dim(inputs, col_first, col_count, 2)
    gate_part = lax.dynamic_slice_in_dim(modulation[2], col_first, col_count, 1)
    mixed = (input_part + gate_part[:, None, :] * summed_part).astype(BF)
    return (mixed, fresh_kv)


def per_device(*arrays):
    clips = arrays[0].shape[0]
    heads_here = arrays[2].shape[2] // HEAD
    patches = lax.axis_size("patch")
    groups = math.gcd(heads_here, patches)
    if clips == 2 and groups == 4 and patches == 4 * groups and lax.axis_size("tp") == 2:
        return spread_heads(groups, *arrays)
    return gather_all(*arrays)


def solution(mesh):
    in_specs = (
        P(None, "patch", None),
        P(),
        P(None, None, "tp"),
        P("tp", None),
        P(),
        P(None, None, "patch", "tp"),
    )
    out_specs = (P(None, "patch", "tp"), P(None, None, "patch", "tp"))
    return jax.shard_map(
        per_device, mesh=mesh, in_specs=in_specs, out_specs=out_specs, check_vma=False
    )
```

```python
import functools
import math

import jax
import jax.numpy as jnp
from jax import lax
from jax.experimental import pallas as pl
from jax.experimental.pallas import tpu as pltpu
from jax.sharding import PartitionSpec as P

HEAD = 128
EXTRA = 16
LOG2E = 1.4426950408889634
SCALE2 = HEAD ** (-0.5) * LOG2E
ORDER = (0, 3, 2, 1)
MIB = 1024 * 1024
BF = jnp.bfloat16
F32 = jnp.float32


SMALL = pl.CostEstimate(flops=1000, bytes_accessed=1000, transcendentals=0)
LARGE = pl.CostEstimate(flops=10**10, bytes_accessed=10**8, transcendentals=0)


def nt(a, b):
    return lax.dot_general(a, b, (((1,), (1,)), ((), ())), preferred_element_type=F32)


def nn(a, b):
    return lax.dot_general(a, b, (((1,), (0,)), ((), ())), preferred_element_type=F32)


def params(mib, **kw):
    return pltpu.CompilerParams(vmem_limit_bytes=mib * MIB, **kw)


def norm_heads(values, gain_row):
    parts = []
    for h in range(values.shape[1] // HEAD):
        v = values[:, h * HEAD : (h + 1) * HEAD]
        square_mean = jnp.mean(v * v, axis=-1, keepdims=True)
        parts.append((v * lax.rsqrt(square_mean + 1e-06) * gain_row).astype(BF))
    return jnp.concatenate(parts, axis=1)


def full(shape):
    return pl.BlockSpec(shape, lambda *_: (0,) * len(shape))


def out_of(shape, dtype=BF):
    return jax.ShapeDtypeStruct(shape, dtype)


ANYWHERE = pl.BlockSpec(memory_space=pltpu.HBM)
SCALARS = pl.BlockSpec(memory_space=pltpu.SMEM)
RESIDENT = pl.BlockSpec(memory_space=pltpu.VMEM)


def copy_all(sems, pairs):
    copies = [pltpu.make_async_copy(a, b, sems.at[i]) for i, (a, b) in enumerate(pairs)]
    for c in copies:
        c.start()
    for c in copies:
        c.wait()


def cut_kernel(width, pos, stale, *rest):
    outs, sems = rest[:-1], rest[-1]
    pairs = []
    for s, out in enumerate(outs):
        cols = pl.ds(pl.multiple_of((pos[0] ^ s) * width, HEAD), width)
        pairs.append((stale.at[:, :, :, cols], out))
    copy_all(sems, pairs)


def cut_stale(pos, stale, groups):
    kv, clips, rows, cols = stale.shape
    width = cols // groups
    return pl.pallas_call(
        functools.partial(cut_kernel, width),
        out_shape=[out_of((kv, clips, rows, width))] * groups,
        in_specs=[SCALARS, ANYWHERE],
        out_specs=[ANYWHERE] * groups,
        scratch_shapes=[pltpu.SemaphoreType.DMA((groups,))],
        compiler_params=params(8),
        name="cut_stale",
    )(pos, stale)


def halves_kernel(block, keys, values, sems):
    copy_all(sems, [(block.at[0], keys), (block.at[1], values)])


def halves(block):
    return pl.pallas_call(
        halves_kernel,
        out_shape=[out_of(block.shape[1:])] * 2,
        in_specs=[ANYWHERE],
        out_specs=[ANYWHERE] * 2,
        scratch_shapes=[pltpu.SemaphoreType.DMA((2,))],
        compiler_params=params(8),
        name="halves",
    )(block)


def pack_kernel(counts, pos, *refs):
    refs, out, sems = list(refs[:-2]), refs[-2], refs[-1]
    pairs, other = [], 1 - pos[2]
    for i, count in enumerate(counts):
        if count == 1:
            pairs.append((refs.pop(0).at[:, other], out.at[i]))
        else:
            pairs += [(refs.pop(0).at[other], out.at[i, kv]) for kv in range(2)]
    copy_all(sems, pairs)


def pack(pos, *blocks):
    rows, width = blocks[0][0].shape[-2:]
    flat = [a for block in blocks for a in block]
    return pl.pallas_call(
        functools.partial(pack_kernel, [len(block) for block in blocks]),
        out_shape=out_of((len(blocks), 2, rows, width)),
        in_specs=[SCALARS] + [ANYWHERE] * len(flat),
        out_specs=ANYWHERE,
        scratch_shapes=[pltpu.SemaphoreType.DMA((len(flat),))],
        compiler_params=params(8),
        name="pack",
    )(pos, *flat)


def query_kernel(groups, per_step, pos, hidden, got, mod, gain, weight, normed, whole, *slots):
    rows = got.shape[0]
    step = pl.program_id(0)

    @pl.when(step == 0)
    def _():
        chunk = 32
        shift, scale = mod[0, pl.ds(pos[2], 1), :], 1.0 + mod[1, pl.ds(pos[2], 1), :]
        for half in range(2):
            for r in range(0, rows, chunk):
                x = hidden[0, r : r + chunk, :] if half == 0 else got[r : r + chunk, :]
                x = x.astype(F32)
                centered = x - jnp.mean(x, axis=-1, keepdims=True)
                var = jnp.mean(centered * centered, axis=-1, keepdims=True)
                y = centered * lax.rsqrt(var + 1e-06) * scale + shift
                normed[half * rows + r : half * rows + r + chunk, :] = y.astype(BF)

    q = norm_heads(nn(normed[...], weight[0]), gain[0:1, :])
    whole[...] = q
    width = q.shape[1] // per_step
    for j in range(per_step):
        part = q[:, j * width : (j + 1) * width]
        slot = (step * per_step + j) ^ pos[0]
        for s in range(groups):

            @pl.when(slot == s)
            def _(s=s, part=part):
                if s < 2:
                    slots[s][...] = part
                else:
                    slots[2 * s - 2][...] = part[:rows]
                    slots[2 * s - 1][...] = part[rows:]


def make_queries(pos, hidden, got, mod, gain, weight, groups):
    rows, width_all = got.shape
    cols = weight.shape[2]
    per_step = 2 if groups % 2 == 0 else 1
    steps = groups // per_step
    width = cols // groups
    wide = width * per_step
    return pl.pallas_call(
        functools.partial(query_kernel, groups, per_step),
        grid_spec=pltpu.PrefetchScalarGridSpec(
            num_scalar_prefetch=1,
            grid=(steps,),
            in_specs=[
                pl.BlockSpec((1, rows, width_all), lambda i, pos: (pos[2], 0, 0)),
                full(got.shape),
                full(mod.shape),
                full(gain.shape),
                pl.BlockSpec((1, width_all, wide), lambda i, pos: (0, 0, i)),
            ],
            out_specs=[
                full((2 * rows, width_all)),
                pl.BlockSpec((2 * rows, wide), lambda i, pos: (0, i)),
            ]
            + [full((2 * rows, width))] * 2
            + [full((rows, width))] * (2 * groups - 4),
        ),
        out_shape=[out_of((2 * rows, width_all)), out_of((2 * rows, cols))]
        + [out_of((2 * rows, width))] * 2
        + [out_of((rows, width))] * (2 * groups - 4),
        compiler_params=params(32),
        cost_estimate=SMALL,
        name="norm_and_queries",
    )(pos, hidden, got, mod, gain, weight)


def fresh_kernel(slot, normed, gain, weight, *refs):
    mine, other = refs[-2:]
    rows = mine.shape[1]
    made = nn(normed[...], weight[0])
    made = norm_heads(made, gain[1:2, :]) if slot == 0 else made.astype(BF)
    mine[0] = made[:rows]
    other[0] = made[rows:]


def make_fresh(slot, normed, gain, weight, before=()):
    rows, width_all = normed.shape
    cols = weight.shape[2]
    block = math.gcd(cols, 768)
    out = pl.BlockSpec((1, rows // 2, block), lambda i: (slot, 0, i))
    return pl.pallas_call(
        functools.partial(fresh_kernel, slot),
        grid=(cols // block,),
        in_specs=[
            full(normed.shape),
            full(gain.shape),
            pl.BlockSpec((1, width_all, block), lambda i: (slot + 1, 0, i)),
        ]
        + [ANYWHERE] * len(before),
        out_specs=[out, out],
        out_shape=[out_of((2, rows // 2, cols))] * 2,
        input_output_aliases={3 + i: i for i in range(len(before))},
        compiler_params=params(32),
        cost_estimate=SMALL,
        name="fresh_keys" if slot == 0 else "fresh_values",
    )(normed, gain, weight, *before)


def place_kernel(pos, mine, got, out, sems):
    clip = pos[2]
    copy_all(sems, [(mine, out.at[:, clip]), (got, out.at[:, 1 - clip])])


def place_fresh(pos, mine, got):
    kv, rows, cols = mine.shape
    return pl.pallas_call(
        place_kernel,
        out_shape=out_of((kv, 2, rows, cols)),
        in_specs=[SCALARS, ANYWHERE, ANYWHERE],
        out_specs=ANYWHERE,
        scratch_shapes=[pltpu.SemaphoreType.DMA((2,))],
        compiler_params=params(8),
        name="place_fresh",
    )(pos, mine, got)


def own_kernel(q, mine, other, acc, top, total):
    rows = mine.shape[1]
    ones = jnp.ones((rows, HEAD), BF)
    heads = q.shape[1] // HEAD
    for j, kv in enumerate((mine, other)):
        here = slice(j * rows, (j + 1) * rows)
        for first in range(0, heads, 3):
            ats = [slice(h * HEAD, (h + 1) * HEAD) for h in range(first, min(first + 3, heads))]
            scores = [nt(q[here, at], kv[0, :, at]) for at in ats]
            values = [jnp.concatenate([kv[1, :, at], ones], axis=1) for at in ats]
            peaks = [jnp.max(sc, axis=-1, keepdims=True) for sc in scores]
            weights = [jnp.exp2((sc - p) * SCALE2).astype(BF) for sc, p in zip(scores, peaks)]
            summed = [nn(w, v) for w, v in zip(weights, values)]
            for at, p, s in zip(ats, peaks, summed):
                acc[here, at] = s[:, :HEAD]
                total[here, at] = s[:, HEAD:]
                top[here, at] = jnp.broadcast_to(p * SCALE2, (rows, HEAD))


def attend_own(queries, mine, other):
    block = math.gcd(queries.shape[1], 768)
    rows, cols = queries.shape
    wide = pl.BlockSpec((rows, block), lambda i: (0, i))
    kv = pl.BlockSpec((2, rows // 2, block), lambda i: (0, 0, i))
    return pl.pallas_call(
        own_kernel,
        grid=(cols // block,),
        in_specs=[wide, kv, kv],
        out_specs=[wide] * 3,
        out_shape=[out_of((rows, cols), F32)] * 3,
        compiler_params=params(24),
        cost_estimate=SMALL,
        name="attend_own",
    )(queries, mine, other)


def group_kernel(part, blocks, places, pos, *refs):
    count = sum(n for n, _ in places)
    queries, refs, outs = refs[:blocks], list(refs[blocks : blocks + count]), refs[blocks + count :]
    outs = [outs[ORDER.index(b)] for b in range(blocks)]
    cached = [[refs.pop(0) for _ in range(n)] for n, _ in places]
    rows, width = queries[-1].shape
    mine = slice(part * rows, (part + 1) * rows)
    clip = pl.ds(pos[2], 1)
    ones = jnp.ones((4 * rows, HEAD), BF)
    heads, levels = width // HEAD, [None] * blocks

    def load(kv, group, at):
        parts = []
        for block, (n, place) in list(zip(cached, places))[4 * group : 4 * group + 4]:
            if place is not None:
                parts.append(block[0][place, kv, :, at])
            elif n == 2:
                parts.append(block[kv][clip, :, at][0])
            else:
                parts.append(block[0][kv, clip, :, at][0])
        return jnp.concatenate(parts, axis=0)

    for h in range(heads):
        at = slice(h * HEAD, (h + 1) * HEAD)
        keys = [load(0, g, at) for g in range(blocks)]
        values = [jnp.concatenate([load(1, g, at), ones], axis=1) for g in range(blocks)]
        for first in range(0, blocks, 2):
            pair = [queries[b][mine if b < 2 else slice(None), at] for b in (first, first + 1)]
            q = jnp.concatenate(pair, axis=0)
            peak = summed = None
            for s in range(blocks):
                sc = nt(q, keys[s])
                if s // 2 == first // 2:
                    halves = [sc[:rows], sc[rows:]]
                    own = [halves[s % 2][:, j * rows : (j + 1) * rows] for j in range(4)]
                    own[part] = jnp.full((rows, rows), -1e30, F32)
                    halves[s % 2] = jnp.concatenate(own, axis=1)
                    sc = jnp.concatenate(halves, axis=0)
                top = jnp.max(sc, axis=-1, keepdims=True)
                top = top if s == 0 else jnp.maximum(peak, top)
                term = nn(jnp.exp2((sc - top) * SCALE2).astype(BF), values[s])
                summed = term if s == 0 else summed * jnp.exp2((peak - top) * SCALE2) + term
                peak = top
            total = summed[:, HEAD:]
            result = (summed[:, :HEAD] / total).astype(BF)
            level_all = peak * SCALE2 + jnp.log2(total)
            for i, b in enumerate((first, first + 1)):
                here = slice(i * rows, (i + 1) * rows)
                outs[b][h * rows : (h + 1) * rows, :] = result[here]
                level = jnp.transpose(level_all[here])[0:EXTRA, :]
                high = level.astype(BF).astype(F32)
                mid = (level - high).astype(BF).astype(F32)
                row = lax.broadcasted_iota(jnp.int32, (EXTRA, HEAD), 0) - 3 * h
                three = jnp.where(row == 0, high, jnp.where(row == 1, mid, level - high - mid))
                levels[b] = three if h == 0 else jnp.where(row < 0, levels[b], three)
    for b in range(blocks):
        outs[b][heads * rows :, :] = levels[b].astype(BF)


def attend_groups(part, pos, queries, cached):
    blocks = len(queries)
    rows, width = queries[-1].shape
    flat = [a for g in cached for a in g]
    arrays = [a for block, _ in flat for a in block]
    places = [(len(block), place) for block, place in flat]
    return pl.pallas_call(
        functools.partial(group_kernel, part, blocks, places),
        in_specs=[SCALARS] + [RESIDENT] * (blocks + len(arrays)),
        out_specs=[RESIDENT] * blocks,
        out_shape=[out_of((rows * width // HEAD + EXTRA, HEAD))] * blocks,
        compiler_params=params(32),
        cost_estimate=SMALL,
        name="attend_groups",
    )(pos, *queries, *arrays)


def out_kernel(part, groups, pos, *refs):
    back = refs[:groups]
    acc, top, total, weight, send, keep, attended = refs[groups:]
    rows = send.shape[0]
    width = acc.shape[1] // groups
    mine = slice(part * rows, (part + 1) * rows)
    for s, block in zip(ORDER, back):
        for h in range(width // HEAD):
            cols = pl.ds(pl.multiple_of((pos[0] ^ s) * width + h * HEAD, HEAD), HEAD)
            three = block[rows * width // HEAD :, :].astype(F32)[3 * h : 3 * h + 3, :]
            level = three[0:1, :] + three[1:2, :] + three[2:3, :]
            level = jnp.transpose(jnp.broadcast_to(level, (rows, HEAD)))
            own = top[mine, cols]
            peak = jnp.maximum(level, own)
            w_own, w_back = jnp.exp2(own - peak), jnp.exp2(level - peak)
            mixed = acc[mine, cols] * w_own + block[h * rows : (h + 1) * rows, :].astype(F32) * w_back
            attended[:, cols] = (mixed / (total[mine, cols] * w_own + w_back)).astype(BF)
    half = weight.shape[1] // 2
    block = math.gcd(half, 768)
    for out, place in ((send, 1 - pos[1]), (keep, pos[1])):
        for i in range(0, half, block):
            cols = pl.ds(pl.multiple_of(place * half + i, HEAD), block)
            out[:, i : i + block] = nn(attended[...], weight[:, cols]).astype(out.dtype)


def project_out(part, pos, back, acc, top, total, weight):
    groups = len(back)
    rows, width_all = acc.shape[0] // 2, acc.shape[1]
    half = (rows, weight.shape[1] // 2)
    return pl.pallas_call(
        functools.partial(out_kernel, part, groups),
        in_specs=[SCALARS] + [RESIDENT] * (groups + 4),
        out_specs=[RESIDENT] * 2,
        out_shape=[out_of(half), out_of(half, F32)],
        scratch_shapes=[pltpu.VMEM((rows, width_all), BF)],
        compiler_params=params(32),
        cost_estimate=LARGE,
        name="merge_and_project",
    )(pos, *back, acc, top, total, weight)


def gated(pos, rows_in, mod, keep, got):
    half = keep.shape[1]
    gate = mod[2, pl.ds(pos[2], 1), pl.ds(pl.multiple_of(pos[1] * half, HEAD), half)]
    return (rows_in.astype(F32) + gate * (keep[...] + got[...].astype(F32))).astype(BF)


def other_rows_kernel(pos, hidden, mod, keep, got, out):
    half = keep.shape[1]
    cols = pl.ds(pl.multiple_of(pos[1] * half, HEAD), half)
    out[...] = gated(pos, hidden[:, cols], mod, keep, got)


def my_rows_kernel(pos, hidden, mod, keep, got, theirs, out):
    half = keep.shape[1]
    cols = pl.ds(pl.multiple_of(pos[1] * half, HEAD), half)
    mine, other = pl.ds(pos[2], 1), pl.ds(1 - pos[2], 1)
    out[mine] = gated(pos, hidden[mine, :, cols][0], mod, keep, got)[None]
    out[other] = theirs[...][None]


def finish(pos, hidden, mod, keep, got, *theirs):
    shape = (2,) * len(theirs) + keep.shape
    return pl.pallas_call(
        my_rows_kernel if theirs else other_rows_kernel,
        in_specs=[SCALARS] + [RESIDENT] * (4 + len(theirs)),
        out_specs=RESIDENT,
        out_shape=out_of(shape),
        compiler_params=params(24),
        cost_estimate=SMALL,
        name="gate_and_add",
    )(pos, hidden, mod, keep, got, *theirs)


def tie(value, *others):
    return lax.optimization_barrier((value, others))[0]


def spread_heads(groups, hidden_states, modulation, qkv_weight, out_weight, qk_gain, stale_kv):
    patches = lax.axis_size("patch")
    inner = patches // groups
    patch = lax.axis_index("patch")
    pos = jnp.stack([patch // inner, lax.axis_index("tp"), patch % 2]).astype(jnp.int32)

    def across(value, bit):
        return lax.ppermute(value, "patch", [(i, i ^ bit) for i in range(patches)])

    def along(value, step):
        return across(value, inner * step)

    weights = jnp.transpose(qkv_weight, (1, 0, 2))
    step = lax.optimization_barrier

    cut = cut_stale(pos, stale_kv, groups)
    near, two, one = cut[:1], [along(cut[2], 2)], [along(cut[1], 1)]
    far_near = [across(near[0], 2)]
    hidden_now = tie(hidden_states, *cut)
    hidden_for = lax.dynamic_index_in_dim(hidden_now, 1 - pos[2], 0, keepdims=False)
    hidden_got = across(hidden_for, 1)
    normed, queries, *slots = make_queries(
        pos, hidden_states, hidden_got, modulation, qk_gain, weights, groups
    )
    normed, queries, slots, near, one, far_near, cut_three = step(
        (normed, queries, slots, near, one, far_near, cut[3])
    )

    three = [along(cut_three, 3)]
    far_one = [across(a, 2) for a in halves(one[0])]
    fresh = make_fresh(0, normed, qk_gain, weights)
    two, far_one, fresh, slots, queries, normed = step(
        (two, far_one, fresh, slots, queries, normed)
    )

    parts = halves(two[0])
    far_two = [across(a, 2) for a in parts]
    asked = [slots[0], along(tie(slots[1], *parts), 1)]
    swap_a = [across(pack(pos, near, far_near, one, far_one), 1)]
    fresh = make_fresh(1, normed, qk_gain, weights, fresh)
    three, far_two, asked, fresh, slots, queries = step(
        (three, far_two, asked, fresh, slots, queries)
    )

    far_three = [across(three[0], 2)]
    their_far = [along(slots[2 * s - 1], s) for s in (2, 3)]
    swap_b = [across(pack(pos, two, far_two, three), 1)]
    own = attend_own(queries, *fresh)
    far_three, their_far, asked, swap_a, swap_b, own, slots = step(
        (far_three, their_far, asked, swap_a, swap_b, own, slots)
    )

    my_far = [along(slots[2 * s - 2], s) for s in (2, 3)]
    their_queries, my_queries = asked + their_far, asked + my_far
    held = [
        [(near, None), (swap_a, 0), (far_near, None), (swap_a, 1)],
        [(one, None), (swap_a, 2), (far_one, None), (swap_a, 3)],
        [(two, None), (swap_b, 0), (far_two, None), (swap_b, 1)],
        [(three, None), (swap_b, 2), (far_three, None), ([across(far_three[0], 1)], None)],
    ]
    theirs = attend_groups(1, pos, their_queries, held)
    theirs, my_queries = step((theirs, my_queries))
    back = [theirs[0]] + [along(a, s) for a, s in zip(theirs[1:], ORDER[1:])]
    my_queries[0] = tie(my_queries[0], theirs)
    mine = attend_groups(0, pos, my_queries, held)
    mine_back = [mine[0]] + [along(a, s) for a, s in zip(mine[1:], ORDER[1:])]
    back[0] = tie(back[0], mine)
    swap = [(0, 1), (1, 0)]
    send, keep = project_out(1, pos, back, *own, out_weight)
    got = lax.ppermute(send, "tp", swap)
    mine_back[0] = tie(mine_back[0], send)

    my_send, my_keep = project_out(0, pos, mine_back, *own, out_weight)
    my_got = lax.ppermute(my_send, "tp", swap)
    fresh_got = across(tie(fresh[1], send), 1)
    fresh_kv = place_fresh(pos, tie(fresh[0], my_send), fresh_got)
    theirs = finish(pos, hidden_got, modulation, tie(keep, my_send), got)
    mixed = finish(pos, hidden_states, modulation, my_keep, my_got, across(theirs, 1))
    return mixed, fresh_kv


def head_norm(values_in, gain_row, heads_here):
    shaped = values_in.reshape(values_in.shape[0], values_in.shape[1], heads_here, HEAD)
    square_mean = jnp.mean(shaped * shaped, axis=-1, keepdims=True)
    return (shaped * lax.rsqrt(square_mean + 1e-06) * gain_row).astype(BF)


def gather_all(hidden_states, modulation, qkv_weight, out_weight, qk_gain, stale_kv):
    clip_count, row_count, width_all = hidden_states.shape
    heads_here = qkv_weight.shape[2] // HEAD
    inputs = hidden_states.astype(F32)
    feature_mean = jnp.mean(inputs, axis=-1, keepdims=True)
    centered = inputs - feature_mean
    feature_var = jnp.mean(centered * centered, axis=-1, keepdims=True)
    normed = (
        centered * lax.rsqrt(feature_var + 1e-06) * (1.0 + modulation[1][:, None, :])
        + modulation[0][:, None, :]
    ).astype(BF)
    projected = jnp.einsum("ctd,dkh->kcth", normed, qkv_weight, preferred_element_type=F32)
    queries = head_norm(projected[0], qk_gain[0], heads_here)
    keys_new = head_norm(projected[1], qk_gain[1], heads_here)
    values_new = projected[2].astype(BF).reshape(clip_count, row_count, heads_here, HEAD)
    fresh_kv = jnp.stack(
        [keys_new.reshape(clip_count, row_count, -1), values_new.reshape(clip_count, row_count, -1)]
    )
    own_first = lax.axis_index("patch") * row_count
    gathered = lax.all_gather(stale_kv, "patch", axis=2, tiled=True)
    gathered = lax.dynamic_update_slice_in_dim(gathered, fresh_kv, own_first, 2)
    count = gathered.shape[2]
    tile_keys = gathered[0].reshape(clip_count, count, heads_here, HEAD)
    tile_values = gathered[1].reshape(clip_count, count, heads_here, HEAD)
    scores = jnp.einsum("cqhd,ckhd->chqk", queries, tile_keys, preferred_element_type=F32)
    scores = scores * HEAD ** (-0.5)
    expo = jnp.exp(scores - jnp.max(scores, axis=-1, keepdims=True))
    summed = jnp.einsum(
        "chqk,ckhd->chqd", expo.astype(BF), tile_values, preferred_element_type=F32
    )
    attended = (summed / jnp.sum(expo, axis=-1)[..., None]).astype(BF)
    attended = jnp.transpose(attended, (0, 2, 1, 3)).reshape(clip_count, row_count, -1)
    product = jnp.einsum("cth,hd->ctd", attended, out_weight, preferred_element_type=F32)
    col_count = width_all // lax.axis_size("tp")
    col_first = lax.axis_index("tp") * col_count
    summed_part = lax.psum_scatter(
        product.astype(BF), "tp", scatter_dimension=2, tiled=True
    ).astype(F32)
    input_part = lax.dynamic_slice_in_dim(inputs, col_first, col_count, 2)
    gate_part = lax.dynamic_slice_in_dim(modulation[2], col_first, col_count, 1)
    mixed = (input_part + gate_part[:, None, :] * summed_part).astype(BF)
    return (mixed, fresh_kv)


def per_device(*arrays):
    clips = arrays[0].shape[0]
    heads_here = arrays[2].shape[2] // HEAD
    patches = lax.axis_size("patch")
    groups = math.gcd(heads_here, patches)
    if clips == 2 and groups == 4 and patches == 4 * groups and lax.axis_size("tp") == 2:
        return spread_heads(groups, *arrays)
    return gather_all(*arrays)


def solution(mesh):
    in_specs = (
        P(None, "patch", None),
        P(),
        P(None, None, "tp"),
        P("tp", None),
        P(),
        P(None, None, "patch", "tp"),
    )
    out_specs = (P(None, "patch", "tp"), P(None, None, "patch", "tp"))
    return jax.shard_map(
        per_device, mesh=mesh, in_specs=in_specs, out_specs=out_specs, check_vma=False
    )
```

```python
import functools
import math

import jax
import jax.numpy as jnp
from jax import lax
from jax.experimental import pallas as pl
from jax.experimental.pallas import tpu as pltpu
from jax.sharding import PartitionSpec as P

HEAD = 128
EXTRA = 16
LOG2E = 1.4426950408889634
SCALE2 = HEAD ** (-0.5) * LOG2E
ORDER = (0, 3, 2, 1)
MIB = 1024 * 1024
BF = jnp.bfloat16
F32 = jnp.float32


SMALL = pl.CostEstimate(flops=1000, bytes_accessed=1000, transcendentals=0)
LARGE = pl.CostEstimate(flops=10**10, bytes_accessed=10**8, transcendentals=0)


def nt(a, b):
    return lax.dot_general(a, b, (((1,), (1,)), ((), ())), preferred_element_type=F32)


def nn(a, b):
    return lax.dot_general(a, b, (((1,), (0,)), ((), ())), preferred_element_type=F32)


def params(mib, **kw):
    return pltpu.CompilerParams(vmem_limit_bytes=mib * MIB, **kw)


def norm_heads(values, gain_row):
    parts = []
    for h in range(values.shape[1] // HEAD):
        v = values[:, h * HEAD : (h + 1) * HEAD]
        square_mean = jnp.mean(v * v, axis=-1, keepdims=True)
        parts.append((v * lax.rsqrt(square_mean + 1e-06) * gain_row).astype(BF))
    return jnp.concatenate(parts, axis=1)


def full(shape):
    return pl.BlockSpec(shape, lambda *_: (0,) * len(shape))


def out_of(shape, dtype=BF):
    return jax.ShapeDtypeStruct(shape, dtype)


ANYWHERE = pl.BlockSpec(memory_space=pltpu.HBM)
SCALARS = pl.BlockSpec(memory_space=pltpu.SMEM)
RESIDENT = pl.BlockSpec(memory_space=pltpu.VMEM)


def copy_all(sems, pairs):
    copies = [pltpu.make_async_copy(a, b, sems.at[i]) for i, (a, b) in enumerate(pairs)]
    for c in copies:
        c.start()
    for c in copies:
        c.wait()


def cut_kernel(width, pos, stale, *outs):
    for s, out in enumerate(outs):
        out[...] = stale[:, :, :, pl.ds(pl.multiple_of((pos[0] ^ s) * width, HEAD), width)]


def cut_stale(pos, stale, groups):
    kv, clips, rows, cols = stale.shape
    width = cols // groups
    return pl.pallas_call(
        functools.partial(cut_kernel, width),
        out_shape=[out_of((kv, clips, rows, width))] * groups,
        in_specs=[SCALARS, RESIDENT],
        out_specs=[RESIDENT] * groups,
        compiler_params=params(8),
        name="cut_stale",
    )(pos, stale)


def halves_kernel(block, keys, values):
    keys[...] = block[0]
    values[...] = block[1]


def halves(block):
    return pl.pallas_call(
        halves_kernel,
        out_shape=[out_of(block.shape[1:])] * 2,
        in_specs=[RESIDENT],
        out_specs=[RESIDENT] * 2,
        compiler_params=params(8),
        name="halves",
    )(block)


def pack_kernel(counts, pos, *refs):
    refs, out = list(refs[:-1]), refs[-1]
    other = pl.ds(1 - pos[2], 1)
    for i, count in enumerate(counts):
        if count == 1:
            out[i] = refs.pop(0)[:, other][:, 0]
        else:
            for kv in range(2):
                out[i, kv] = refs.pop(0)[other][0]


def pack(pos, *blocks):
    rows, width = blocks[0][0].shape[-2:]
    flat = [a for block in blocks for a in block]
    return pl.pallas_call(
        functools.partial(pack_kernel, [len(block) for block in blocks]),
        out_shape=out_of((len(blocks), 2, rows, width)),
        in_specs=[SCALARS] + [RESIDENT] * len(flat),
        out_specs=RESIDENT,
        compiler_params=params(8),
        name="pack",
    )(pos, *flat)


def query_kernel(groups, per_step, pos, hidden, got, mod, gain, weight, normed, whole, *slots):
    rows = got.shape[0]
    step = pl.program_id(0)

    @pl.when(step == 0)
    def _():
        chunk = 32
        shift, scale = mod[0, pl.ds(pos[2], 1), :], 1.0 + mod[1, pl.ds(pos[2], 1), :]
        for half in range(2):
            for r in range(0, rows, chunk):
                x = hidden[0, r : r + chunk, :] if half == 0 else got[r : r + chunk, :]
                x = x.astype(F32)
                centered = x - jnp.mean(x, axis=-1, keepdims=True)
                var = jnp.mean(centered * centered, axis=-1, keepdims=True)
                y = centered * lax.rsqrt(var + 1e-06) * scale + shift
                normed[half * rows + r : half * rows + r + chunk, :] = y.astype(BF)

    q = norm_heads(nn(normed[...], weight[0]), gain[0:1, :])
    whole[...] = q
    width = q.shape[1] // per_step
    for j in range(per_step):
        part = q[:, j * width : (j + 1) * width]
        slot = (step * per_step + j) ^ pos[0]
        for s in range(groups):

            @pl.when(slot == s)
            def _(s=s, part=part):
                if s < 2:
                    slots[s][...] = part
                else:
                    slots[2 * s - 2][...] = part[:rows]
                    slots[2 * s - 1][...] = part[rows:]


def make_queries(pos, hidden, got, mod, gain, weight, groups):
    rows, width_all = got.shape
    cols = weight.shape[2]
    per_step = 2 if groups % 2 == 0 else 1
    steps = groups // per_step
    width = cols // groups
    wide = width * per_step
    return pl.pallas_call(
        functools.partial(query_kernel, groups, per_step),
        grid_spec=pltpu.PrefetchScalarGridSpec(
            num_scalar_prefetch=1,
            grid=(steps,),
            in_specs=[
                pl.BlockSpec((1, rows, width_all), lambda i, pos: (pos[2], 0, 0)),
                full(got.shape),
                full(mod.shape),
                full(gain.shape),
                pl.BlockSpec((1, width_all, wide), lambda i, pos: (0, 0, i)),
            ],
            out_specs=[
                full((2 * rows, width_all)),
                pl.BlockSpec((2 * rows, wide), lambda i, pos: (0, i)),
            ]
            + [full((2 * rows, width))] * 2
            + [full((rows, width))] * (2 * groups - 4),
        ),
        out_shape=[out_of((2 * rows, width_all)), out_of((2 * rows, cols))]
        + [out_of((2 * rows, width))] * 2
        + [out_of((rows, width))] * (2 * groups - 4),
        compiler_params=params(32),
        cost_estimate=SMALL,
        name="norm_and_queries",
    )(pos, hidden, got, mod, gain, weight)


def fresh_kernel(slot, normed, gain, weight, *refs):
    mine, other = refs[-2:]
    rows = mine.shape[1]
    made = nn(normed[...], weight[0])
    made = norm_heads(made, gain[1:2, :]) if slot == 0 else made.astype(BF)
    mine[0] = made[:rows]
    other[0] = made[rows:]


def make_fresh(slot, normed, gain, weight, before=()):
    rows, width_all = normed.shape
    cols = weight.shape[2]
    block = math.gcd(cols, 768)
    out = pl.BlockSpec((1, rows // 2, block), lambda i: (slot, 0, i))
    return pl.pallas_call(
        functools.partial(fresh_kernel, slot),
        grid=(cols // block,),
        in_specs=[
            full(normed.shape),
            full(gain.shape),
            pl.BlockSpec((1, width_all, block), lambda i: (slot + 1, 0, i)),
        ]
        + [ANYWHERE] * len(before),
        out_specs=[out, out],
        out_shape=[out_of((2, rows // 2, cols))] * 2,
        input_output_aliases={3 + i: i for i in range(len(before))},
        compiler_params=params(32),
        cost_estimate=SMALL,
        name="fresh_keys" if slot == 0 else "fresh_values",
    )(normed, gain, weight, *before)


def place_kernel(pos, mine, got, out, sems):
    clip = pos[2]
    copy_all(sems, [(mine, out.at[:, clip]), (got, out.at[:, 1 - clip])])


def place_fresh(pos, mine, got):
    kv, rows, cols = mine.shape
    return pl.pallas_call(
        place_kernel,
        out_shape=out_of((kv, 2, rows, cols)),
        in_specs=[SCALARS, ANYWHERE, ANYWHERE],
        out_specs=ANYWHERE,
        scratch_shapes=[pltpu.SemaphoreType.DMA((2,))],
        compiler_params=params(8),
        name="place_fresh",
    )(pos, mine, got)


def own_kernel(q, mine, other, acc, top, total):
    rows = mine.shape[1]
    ones = jnp.ones((rows, HEAD), BF)
    heads = q.shape[1] // HEAD
    for j, kv in enumerate((mine, other)):
        here = slice(j * rows, (j + 1) * rows)
        for first in range(0, heads, 3):
            ats = [slice(h * HEAD, (h + 1) * HEAD) for h in range(first, min(first + 3, heads))]
            scores = [nt(q[here, at], kv[0, :, at]) for at in ats]
            values = [jnp.concatenate([kv[1, :, at], ones], axis=1) for at in ats]
            peaks = [jnp.max(sc, axis=-1, keepdims=True) for sc in scores]
            weights = [jnp.exp2((sc - p) * SCALE2).astype(BF) for sc, p in zip(scores, peaks)]
            summed = [nn(w, v) for w, v in zip(weights, values)]
            for at, p, s in zip(ats, peaks, summed):
                acc[here, at] = s[:, :HEAD]
                total[here, at] = s[:, HEAD:]
                top[here, at] = jnp.broadcast_to(p * SCALE2, (rows, HEAD))


def attend_own(queries, mine, other):
    block = math.gcd(queries.shape[1], 768)
    rows, cols = queries.shape
    wide = pl.BlockSpec((rows, block), lambda i: (0, i))
    kv = pl.BlockSpec((2, rows // 2, block), lambda i: (0, 0, i))
    return pl.pallas_call(
        own_kernel,
        grid=(cols // block,),
        in_specs=[wide, kv, kv],
        out_specs=[wide] * 3,
        out_shape=[out_of((rows, cols), F32)] * 3,
        compiler_params=params(24),
        cost_estimate=SMALL,
        name="attend_own",
    )(queries, mine, other)


def group_kernel(part, blocks, places, pos, *refs):
    count = sum(n for n, _ in places)
    queries, refs, outs = refs[:blocks], list(refs[blocks : blocks + count]), refs[blocks + count :]
    outs = [outs[ORDER.index(b)] for b in range(blocks)]
    cached = [[refs.pop(0) for _ in range(n)] for n, _ in places]
    rows, width = queries[-1].shape
    mine = slice(part * rows, (part + 1) * rows)
    clip = pl.ds(pos[2], 1)
    ones = jnp.ones((4 * rows, HEAD), BF)
    heads, levels = width // HEAD, [None] * blocks

    def load(kv, group, at):
        parts = []
        for block, (n, place) in list(zip(cached, places))[4 * group : 4 * group + 4]:
            if place is not None:
                parts.append(block[0][place, kv, :, at])
            elif n == 2:
                parts.append(block[kv][clip, :, at][0])
            else:
                parts.append(block[0][kv, clip, :, at][0])
        return jnp.concatenate(parts, axis=0)

    for h in range(heads):
        at = slice(h * HEAD, (h + 1) * HEAD)
        keys = [load(0, g, at) for g in range(blocks)]
        values = [jnp.concatenate([load(1, g, at), ones], axis=1) for g in range(blocks)]
        for first in range(0, blocks, 2):
            pair = [queries[b][mine if b < 2 else slice(None), at] for b in (first, first + 1)]
            q = jnp.concatenate(pair, axis=0)
            peak = summed = None
            for s in range(blocks):
                sc = nt(q, keys[s])
                if s // 2 == first // 2:
                    halves = [sc[:rows], sc[rows:]]
                    own = [halves[s % 2][:, j * rows : (j + 1) * rows] for j in range(4)]
                    own[part] = jnp.full((rows, rows), -1e30, F32)
                    halves[s % 2] = jnp.concatenate(own, axis=1)
                    sc = jnp.concatenate(halves, axis=0)
                top = jnp.max(sc, axis=-1, keepdims=True)
                top = top if s == 0 else jnp.maximum(peak, top)
                term = nn(jnp.exp2((sc - top) * SCALE2).astype(BF), values[s])
                summed = term if s == 0 else summed * jnp.exp2((peak - top) * SCALE2) + term
                peak = top
            total = summed[:, HEAD:]
            result = (summed[:, :HEAD] / total).astype(BF)
            level_all = peak * SCALE2 + jnp.log2(total)
            for i, b in enumerate((first, first + 1)):
                here = slice(i * rows, (i + 1) * rows)
                outs[b][h * rows : (h + 1) * rows, :] = result[here]
                level = jnp.transpose(level_all[here])[0:EXTRA, :]
                high = level.astype(BF).astype(F32)
                mid = (level - high).astype(BF).astype(F32)
                row = lax.broadcasted_iota(jnp.int32, (EXTRA, HEAD), 0) - 3 * h
                three = jnp.where(row == 0, high, jnp.where(row == 1, mid, level - high - mid))
                levels[b] = three if h == 0 else jnp.where(row < 0, levels[b], three)
    for b in range(blocks):
        outs[b][heads * rows :, :] = levels[b].astype(BF)


def attend_groups(part, pos, queries, cached):
    blocks = len(queries)
    rows, width = queries[-1].shape
    flat = [a for g in cached for a in g]
    arrays = [a for block, _ in flat for a in block]
    places = [(len(block), place) for block, place in flat]
    return pl.pallas_call(
        functools.partial(group_kernel, part, blocks, places),
        in_specs=[SCALARS] + [RESIDENT] * (blocks + len(arrays)),
        out_specs=[RESIDENT] * blocks,
        out_shape=[out_of((rows * width // HEAD + EXTRA, HEAD))] * blocks,
        compiler_params=params(32),
        cost_estimate=SMALL,
        name="attend_groups",
    )(pos, *queries, *arrays)


def out_kernel(part, groups, pos, *refs):
    back = refs[:groups]
    acc, top, total, weight, send, attended = refs[groups:]
    rows = send.shape[0]
    width = acc.shape[1] // groups
    mine = slice(part * rows, (part + 1) * rows)
    for s, block in zip(ORDER, back):
        for h in range(width // HEAD):
            cols = pl.ds(pl.multiple_of((pos[0] ^ s) * width + h * HEAD, HEAD), HEAD)
            three = block[rows * width // HEAD :, :].astype(F32)[3 * h : 3 * h + 3, :]
            level = three[0:1, :] + three[1:2, :] + three[2:3, :]
            level = jnp.transpose(jnp.broadcast_to(level, (rows, HEAD)))
            own = top[mine, cols]
            peak = jnp.maximum(level, own)
            w_own, w_back = jnp.exp2(own - peak), jnp.exp2(level - peak)
            mixed = acc[mine, cols] * w_own + block[h * rows : (h + 1) * rows, :].astype(F32) * w_back
            attended[:, cols] = (mixed / (total[mine, cols] * w_own + w_back)).astype(BF)
    project(attended, weight, 1 - pos[1], send)


def project(attended, weight, place, out):
    half = out.shape[1]
    block = math.gcd(half, 768)
    for i in range(0, half, block):
        cols = pl.ds(pl.multiple_of(place * half + i, HEAD), block)
        out[:, i : i + block] = nn(attended[...], weight[:, cols]).astype(out.dtype)


def project_out(part, pos, back, acc, top, total, weight):
    groups = len(back)
    rows, width_all = acc.shape[0] // 2, acc.shape[1]
    return pl.pallas_call(
        functools.partial(out_kernel, part, groups),
        in_specs=[SCALARS] + [RESIDENT] * (groups + 4),
        out_specs=[RESIDENT] * 2,
        out_shape=[out_of((rows, weight.shape[1] // 2)), out_of((rows, width_all))],
        compiler_params=params(32),
        cost_estimate=LARGE,
        name="merge_and_project",
    )(pos, *back, acc, top, total, weight)


def keep_kernel(pos, attended, weight, keep):
    project(attended, weight, pos[1], keep)


def project_kept(pos, attended, weight):
    return pl.pallas_call(
        keep_kernel,
        in_specs=[SCALARS] + [RESIDENT] * 2,
        out_specs=RESIDENT,
        out_shape=out_of((attended.shape[0], weight.shape[1] // 2), F32),
        compiler_params=params(32),
        cost_estimate=SMALL,
        name="project_kept",
    )(pos, attended, weight)


def gated(pos, rows_in, mod, keep, got):
    half = keep.shape[1]
    gate = mod[2, pl.ds(pos[2], 1), pl.ds(pl.multiple_of(pos[1] * half, HEAD), half)]
    return (rows_in.astype(F32) + gate * (keep[...] + got[...].astype(F32))).astype(BF)


def other_rows_kernel(pos, hidden, mod, keep, got, out):
    half = keep.shape[1]
    cols = pl.ds(pl.multiple_of(pos[1] * half, HEAD), half)
    out[...] = gated(pos, hidden[:, cols], mod, keep, got)


def my_rows_kernel(pos, hidden, mod, keep, got, theirs, out, rows, sems):
    half = keep.shape[1]
    mine, other = pos[2], 1 - pos[2]
    copies = [pltpu.make_async_copy(theirs, out.at[other], sems.at[0])]
    copies[0].start()
    block = half // 2
    for i in range(2):
        here = slice(i * block, (i + 1) * block)
        cols = pl.ds(pl.multiple_of(pos[1] * half + i * block, HEAD), block)
        gate = mod[2, pl.ds(mine, 1), cols]
        total = keep[:, here] + got[:, here].astype(F32)
        before = hidden[pl.ds(mine, 1), :, cols][0].astype(F32)
        rows[:, here] = (before + gate * total).astype(BF)
        copy = pltpu.make_async_copy(rows.at[:, here], out.at[mine, :, here], sems.at[i + 1])
        copy.start()
        copies.append(copy)
    for copy in copies:
        copy.wait()


def finish(pos, hidden, mod, keep, got, *theirs):
    scratch = [pltpu.VMEM(keep.shape, BF), pltpu.SemaphoreType.DMA((3,))]
    return pl.pallas_call(
        my_rows_kernel if theirs else other_rows_kernel,
        in_specs=[SCALARS] + [RESIDENT] * (4 + len(theirs)),
        out_specs=ANYWHERE if theirs else RESIDENT,
        out_shape=out_of((2,) * len(theirs) + keep.shape),
        scratch_shapes=scratch if theirs else [],
        compiler_params=params(24),
        cost_estimate=SMALL,
        name="gate_and_add",
    )(pos, hidden, mod, keep, got, *theirs)


def tie(value, *others):
    return lax.optimization_barrier((value, others))[0]


def spread_heads(groups, hidden_states, modulation, qkv_weight, out_weight, qk_gain, stale_kv):
    patches = lax.axis_size("patch")
    inner = patches // groups
    patch = lax.axis_index("patch")
    pos = jnp.stack([patch // inner, lax.axis_index("tp"), patch % 2]).astype(jnp.int32)

    def across(value, bit):
        return lax.ppermute(value, "patch", [(i, i ^ bit) for i in range(patches)])

    def along(value, step):
        return across(value, inner * step)

    weights = jnp.transpose(qkv_weight, (1, 0, 2))
    step = lax.optimization_barrier

    cut = cut_stale(pos, stale_kv, groups)
    near, two, one = cut[:1], [along(cut[2], 2)], [along(cut[1], 1)]
    far_near = [across(near[0], 2)]
    hidden_now = tie(hidden_states, *cut)
    hidden_for = lax.dynamic_index_in_dim(hidden_now, 1 - pos[2], 0, keepdims=False)
    hidden_got = across(hidden_for, 1)
    normed, queries, *slots = make_queries(
        pos, hidden_states, hidden_got, modulation, qk_gain, weights, groups
    )
    normed, queries, slots, near, one, far_near, cut_three = step(
        (normed, queries, slots, near, one, far_near, cut[3])
    )

    three = [along(cut_three, 3)]
    far_one = [across(a, 2) for a in halves(one[0])]
    fresh = make_fresh(0, normed, qk_gain, weights)
    two, far_one, fresh, slots, queries, normed = step(
        (two, far_one, fresh, slots, queries, normed)
    )

    parts = halves(two[0])
    far_two = [across(a, 2) for a in parts]
    asked = [slots[0], along(tie(slots[1], *parts), 1)]
    swap_a = [across(pack(pos, near, far_near, one, far_one), 1)]
    fresh = make_fresh(1, normed, qk_gain, weights, fresh)
    three, far_two, asked, fresh, slots, queries = step(
        (three, far_two, asked, fresh, slots, queries)
    )

    far_three = [across(three[0], 2)]
    their_far = [along(slots[2 * s - 1], s) for s in (2, 3)]
    swap_b = [across(pack(pos, two, far_two, three), 1)]
    own = attend_own(queries, *fresh)
    far_three, their_far, asked, swap_a, swap_b, own, slots = step(
        (far_three, their_far, asked, swap_a, swap_b, own, slots)
    )

    my_far = [along(slots[2 * s - 2], s) for s in (2, 3)]
    their_queries, my_queries = asked + their_far, asked + my_far
    held = [
        [(near, None), (swap_a, 0), (far_near, None), (swap_a, 1)],
        [(one, None), (swap_a, 2), (far_one, None), (swap_a, 3)],
        [(two, None), (swap_b, 0), (far_two, None), (swap_b, 1)],
        [(three, None), (swap_b, 2), (far_three, None), ([across(far_three[0], 1)], None)],
    ]
    theirs = attend_groups(1, pos, their_queries, held)
    theirs, my_queries = step((theirs, my_queries))
    back = [theirs[0]] + [along(a, s) for a, s in zip(theirs[1:], ORDER[1:])]
    my_queries[0] = tie(my_queries[0], theirs)
    mine = attend_groups(0, pos, my_queries, held)
    mine_back = [mine[0]] + [along(a, s) for a, s in zip(mine[1:], ORDER[1:])]
    back[0] = tie(back[0], mine)
    swap = [(0, 1), (1, 0)]
    send, attended = project_out(1, pos, back, *own, out_weight)
    got = lax.ppermute(send, "tp", swap)
    mine_back[0] = tie(mine_back[0], send)

    my_send, my_attended = project_out(0, pos, mine_back, *own, out_weight)
    my_got = lax.ppermute(my_send, "tp", swap)
    fresh_got = across(tie(fresh[1], send), 1)
    fresh_kv = place_fresh(pos, tie(fresh[0], my_send), fresh_got)
    keep = project_kept(pos, tie(attended, my_send), out_weight)
    my_keep = project_kept(pos, my_attended, out_weight)
    theirs = finish(pos, hidden_got, modulation, keep, got)
    mixed = finish(pos, hidden_states, modulation, my_keep, my_got, across(theirs, 1))
    return mixed, fresh_kv


def head_norm(values_in, gain_row, heads_here):
    shaped = values_in.reshape(values_in.shape[0], values_in.shape[1], heads_here, HEAD)
    square_mean = jnp.mean(shaped * shaped, axis=-1, keepdims=True)
    return (shaped * lax.rsqrt(square_mean + 1e-06) * gain_row).astype(BF)


def gather_all(hidden_states, modulation, qkv_weight, out_weight, qk_gain, stale_kv):
    clip_count, row_count, width_all = hidden_states.shape
    heads_here = qkv_weight.shape[2] // HEAD
    inputs = hidden_states.astype(F32)
    feature_mean = jnp.mean(inputs, axis=-1, keepdims=True)
    centered = inputs - feature_mean
    feature_var = jnp.mean(centered * centered, axis=-1, keepdims=True)
    normed = (
        centered * lax.rsqrt(feature_var + 1e-06) * (1.0 + modulation[1][:, None, :])
        + modulation[0][:, None, :]
    ).astype(BF)
    projected = jnp.einsum("ctd,dkh->kcth", normed, qkv_weight, preferred_element_type=F32)
    queries = head_norm(projected[0], qk_gain[0], heads_here)
    keys_new = head_norm(projected[1], qk_gain[1], heads_here)
    values_new = projected[2].astype(BF).reshape(clip_count, row_count, heads_here, HEAD)
    fresh_kv = jnp.stack(
        [keys_new.reshape(clip_count, row_count, -1), values_new.reshape(clip_count, row_count, -1)]
    )
    own_first = lax.axis_index("patch") * row_count
    gathered = lax.all_gather(stale_kv, "patch", axis=2, tiled=True)
    gathered = lax.dynamic_update_slice_in_dim(gathered, fresh_kv, own_first, 2)
    count = gathered.shape[2]
    tile_keys = gathered[0].reshape(clip_count, count, heads_here, HEAD)
    tile_values = gathered[1].reshape(clip_count, count, heads_here, HEAD)
    scores = jnp.einsum("cqhd,ckhd->chqk", queries, tile_keys, preferred_element_type=F32)
    scores = scores * HEAD ** (-0.5)
    expo = jnp.exp(scores - jnp.max(scores, axis=-1, keepdims=True))
    summed = jnp.einsum(
        "chqk,ckhd->chqd", expo.astype(BF), tile_values, preferred_element_type=F32
    )
    attended = (summed / jnp.sum(expo, axis=-1)[..., None]).astype(BF)
    attended = jnp.transpose(attended, (0, 2, 1, 3)).reshape(clip_count, row_count, -1)
    product = jnp.einsum("cth,hd->ctd", attended, out_weight, preferred_element_type=F32)
    col_count = width_all // lax.axis_size("tp")
    col_first = lax.axis_index("tp") * col_count
    summed_part = lax.psum_scatter(
        product.astype(BF), "tp", scatter_dimension=2, tiled=True
    ).astype(F32)
    input_part = lax.dynamic_slice_in_dim(inputs, col_first, col_count, 2)
    gate_part = lax.dynamic_slice_in_dim(modulation[2], col_first, col_count, 1)
    mixed = (input_part + gate_part[:, None, :] * summed_part).astype(BF)
    return (mixed, fresh_kv)


def per_device(*arrays):
    clips = arrays[0].shape[0]
    heads_here = arrays[2].shape[2] // HEAD
    patches = lax.axis_size("patch")
    groups = math.gcd(heads_here, patches)
    if clips == 2 and groups == 4 and heads_here <= 5 * groups and patches == 4 * groups and lax.axis_size("tp") == 2:
        return spread_heads(groups, *arrays)
    return gather_all(*arrays)


def solution(mesh):
    in_specs = (
        P(None, "patch", None),
        P(),
        P(None, None, "tp"),
        P("tp", None),
        P(),
        P(None, None, "patch", "tp"),
    )
    out_specs = (P(None, "patch", "tp"), P(None, None, "patch", "tp"))
    return jax.shard_map(
        per_device, mesh=mesh, in_specs=in_specs, out_specs=out_specs, check_vma=False
    )
```

```python
import functools
import math

import jax
import jax.numpy as jnp
from jax import lax
from jax.experimental import pallas as pl
from jax.experimental.pallas import tpu as pltpu
from jax.sharding import PartitionSpec as P

HEAD = 128
EXTRA = 16
LOG2E = 1.4426950408889634
SCALE2 = HEAD ** (-0.5) * LOG2E
ORDER = ((0, 1, 3, 2), (0, 3, 2, 1))
MIB = 1024 * 1024
BF = jnp.bfloat16
F32 = jnp.float32


SMALL = pl.CostEstimate(flops=1000, bytes_accessed=1000, transcendentals=0)
LARGE = pl.CostEstimate(flops=10**10, bytes_accessed=10**8, transcendentals=0)


def nt(a, b):
    return lax.dot_general(a, b, (((1,), (1,)), ((), ())), preferred_element_type=F32)


def nn(a, b):
    return lax.dot_general(a, b, (((1,), (0,)), ((), ())), preferred_element_type=F32)


def params(mib, **kw):
    return pltpu.CompilerParams(vmem_limit_bytes=mib * MIB, **kw)


def norm_heads(values, gain_row):
    parts = []
    for h in range(values.shape[1] // HEAD):
        v = values[:, h * HEAD : (h + 1) * HEAD]
        square_mean = jnp.mean(v * v, axis=-1, keepdims=True)
        parts.append((v * lax.rsqrt(square_mean + 1e-06) * gain_row).astype(BF))
    return jnp.concatenate(parts, axis=1)


def full(shape):
    return pl.BlockSpec(shape, lambda *_: (0,) * len(shape))


def out_of(shape, dtype=BF):
    return jax.ShapeDtypeStruct(shape, dtype)


ANYWHERE = pl.BlockSpec(memory_space=pltpu.HBM)
SCALARS = pl.BlockSpec(memory_space=pltpu.SMEM)
RESIDENT = pl.BlockSpec(memory_space=pltpu.VMEM)


def copy_all(sems, pairs):
    copies = [pltpu.make_async_copy(a, b, sems.at[i]) for i, (a, b) in enumerate(pairs)]
    for c in copies:
        c.start()
    for c in copies:
        c.wait()


def cut_kernel(width, pos, stale, *outs):
    for s, out in enumerate(outs):
        out[...] = stale[:, :, :, pl.ds(pl.multiple_of((pos[0] ^ s) * width, HEAD), width)]


def cut_stale(pos, stale, groups):
    kv, clips, rows, cols = stale.shape
    width = cols // groups
    return pl.pallas_call(
        functools.partial(cut_kernel, width),
        out_shape=[out_of((kv, clips, rows, width))] * groups,
        in_specs=[SCALARS, RESIDENT],
        out_specs=[RESIDENT] * groups,
        compiler_params=params(8),
        name="cut_stale",
    )(pos, stale)


def halves_kernel(block, keys, values):
    keys[...] = block[0]
    values[...] = block[1]


def halves(block):
    return pl.pallas_call(
        halves_kernel,
        out_shape=[out_of(block.shape[1:])] * 2,
        in_specs=[RESIDENT],
        out_specs=[RESIDENT] * 2,
        compiler_params=params(8),
        name="halves",
    )(block)


def pack_kernel(counts, pos, *refs):
    refs, out = list(refs[:-1]), refs[-1]
    other = pl.ds(1 - pos[2], 1)
    for i, count in enumerate(counts):
        if count == 1:
            out[i] = refs.pop(0)[:, other][:, 0]
        else:
            for kv in range(2):
                out[i, kv] = refs.pop(0)[other][0]


def pack(pos, *blocks):
    rows, width = blocks[0][0].shape[-2:]
    flat = [a for block in blocks for a in block]
    return pl.pallas_call(
        functools.partial(pack_kernel, [len(block) for block in blocks]),
        out_shape=out_of((len(blocks), 2, rows, width)),
        in_specs=[SCALARS] + [RESIDENT] * len(flat),
        out_specs=RESIDENT,
        compiler_params=params(8),
        name="pack",
    )(pos, *flat)


def query_kernel(groups, per_step, pos, hidden, got, mod, gain, weight, normed, whole, *slots):
    rows = got.shape[0]
    step = pl.program_id(0)

    @pl.when(step == 0)
    def _():
        chunk = 32
        shift, scale = mod[0, pl.ds(pos[2], 1), :], 1.0 + mod[1, pl.ds(pos[2], 1), :]
        for half in range(2):
            for r in range(0, rows, chunk):
                x = hidden[0, r : r + chunk, :] if half == 0 else got[r : r + chunk, :]
                x = x.astype(F32)
                centered = x - jnp.mean(x, axis=-1, keepdims=True)
                var = jnp.mean(centered * centered, axis=-1, keepdims=True)
                y = centered * lax.rsqrt(var + 1e-06) * scale + shift
                normed[half * rows + r : half * rows + r + chunk, :] = y.astype(BF)

    q = norm_heads(nn(normed[...], weight[0]), gain[0:1, :])
    whole[...] = q
    width = q.shape[1] // per_step
    for j in range(per_step):
        part = q[:, j * width : (j + 1) * width]
        slot = (step * per_step + j) ^ pos[0]
        for s in range(groups):

            @pl.when(slot == s)
            def _(s=s, part=part):
                if s < 2:
                    slots[s][...] = part
                else:
                    slots[2 * s - 2][...] = part[:rows]
                    slots[2 * s - 1][...] = part[rows:]


def make_queries(pos, hidden, got, mod, gain, weight, groups):
    rows, width_all = got.shape
    cols = weight.shape[2]
    per_step = 2 if groups % 2 == 0 else 1
    steps = groups // per_step
    width = cols // groups
    wide = width * per_step
    return pl.pallas_call(
        functools.partial(query_kernel, groups, per_step),
        grid_spec=pltpu.PrefetchScalarGridSpec(
            num_scalar_prefetch=1,
            grid=(steps,),
            in_specs=[
                pl.BlockSpec((1, rows, width_all), lambda i, pos: (pos[2], 0, 0)),
                full(got.shape),
                full(mod.shape),
                full(gain.shape),
                pl.BlockSpec((1, width_all, wide), lambda i, pos: (0, 0, i)),
            ],
            out_specs=[
                full((2 * rows, width_all)),
                pl.BlockSpec((2 * rows, wide), lambda i, pos: (0, i)),
            ]
            + [full((2 * rows, width))] * 2
            + [full((rows, width))] * (2 * groups - 4),
        ),
        out_shape=[out_of((2 * rows, width_all)), out_of((2 * rows, cols))]
        + [out_of((2 * rows, width))] * 2
        + [out_of((rows, width))] * (2 * groups - 4),
        compiler_params=params(32),
        cost_estimate=SMALL,
        name="norm_and_queries",
    )(pos, hidden, got, mod, gain, weight)


def fresh_kernel(slot, normed, gain, weight, *refs):
    mine, other = refs[-2:]
    rows = mine.shape[1]
    made = nn(normed[...], weight[0])
    made = norm_heads(made, gain[1:2, :]) if slot == 0 else made.astype(BF)
    mine[0] = made[:rows]
    other[0] = made[rows:]


def make_fresh(slot, normed, gain, weight, before=()):
    rows, width_all = normed.shape
    cols = weight.shape[2]
    block = math.gcd(cols, 768)
    out = pl.BlockSpec((1, rows // 2, block), lambda i: (slot, 0, i))
    return pl.pallas_call(
        functools.partial(fresh_kernel, slot),
        grid=(cols // block,),
        in_specs=[
            full(normed.shape),
            full(gain.shape),
            pl.BlockSpec((1, width_all, block), lambda i: (slot + 1, 0, i)),
        ]
        + [ANYWHERE] * len(before),
        out_specs=[out, out],
        out_shape=[out_of((2, rows // 2, cols))] * 2,
        input_output_aliases={3 + i: i for i in range(len(before))},
        compiler_params=params(32),
        cost_estimate=SMALL,
        name="fresh_keys" if slot == 0 else "fresh_values",
    )(normed, gain, weight, *before)


def place_kernel(pos, mine, got, out, sems):
    clip = pos[2]
    copy_all(sems, [(mine, out.at[:, clip]), (got, out.at[:, 1 - clip])])


def place_fresh(pos, mine, got):
    kv, rows, cols = mine.shape
    return pl.pallas_call(
        place_kernel,
        out_shape=out_of((kv, 2, rows, cols)),
        in_specs=[SCALARS, ANYWHERE, ANYWHERE],
        out_specs=ANYWHERE,
        scratch_shapes=[pltpu.SemaphoreType.DMA((2,))],
        compiler_params=params(8),
        name="place_fresh",
    )(pos, mine, got)


def own_kernel(q, mine, other, acc, top, total):
    rows = mine.shape[1]
    ones = jnp.ones((rows, HEAD), BF)
    heads = q.shape[1] // HEAD
    for j, kv in enumerate((mine, other)):
        here = slice(j * rows, (j + 1) * rows)
        for first in range(0, heads, 3):
            ats = [slice(h * HEAD, (h + 1) * HEAD) for h in range(first, min(first + 3, heads))]
            scores = [nt(q[here, at], kv[0, :, at]) for at in ats]
            values = [jnp.concatenate([kv[1, :, at], ones], axis=1) for at in ats]
            peaks = [jnp.max(sc, axis=-1, keepdims=True) for sc in scores]
            weights = [jnp.exp2((sc - p) * SCALE2).astype(BF) for sc, p in zip(scores, peaks)]
            summed = [nn(w, v) for w, v in zip(weights, values)]
            for at, p, s in zip(ats, peaks, summed):
                acc[here, at] = s[:, :HEAD]
                total[here, at] = s[:, HEAD:]
                top[here, at] = jnp.broadcast_to(p * SCALE2, (rows, HEAD))


def attend_own(queries, mine, other):
    block = math.gcd(queries.shape[1], 768)
    rows, cols = queries.shape
    wide = pl.BlockSpec((rows, block), lambda i: (0, i))
    kv = pl.BlockSpec((2, rows // 2, block), lambda i: (0, 0, i))
    return pl.pallas_call(
        own_kernel,
        grid=(cols // block,),
        in_specs=[wide, kv, kv],
        out_specs=[wide] * 3,
        out_shape=[out_of((rows, cols), F32)] * 3,
        compiler_params=params(24),
        cost_estimate=SMALL,
        name="attend_own",
    )(queries, mine, other)


def group_kernel(part, blocks, places, pos, *refs):
    count = sum(n for n, _ in places)
    queries, refs, outs = refs[:blocks], list(refs[blocks : blocks + count]), refs[blocks + count :]
    outs = [outs[ORDER[part].index(b)] for b in range(blocks)]
    cached = [[refs.pop(0) for _ in range(n)] for n, _ in places]
    rows, width = queries[-1].shape
    mine = slice(part * rows, (part + 1) * rows)
    clip = pl.ds(pos[2], 1)
    ones = jnp.ones((4 * rows, HEAD), BF)
    heads, levels = width // HEAD, [None] * blocks

    def load(kv, group, at):
        parts = []
        for block, (n, place) in list(zip(cached, places))[4 * group : 4 * group + 4]:
            if place is not None:
                parts.append(block[0][place, kv, :, at])
            elif n == 2:
                parts.append(block[kv][clip, :, at][0])
            else:
                parts.append(block[0][kv, clip, :, at][0])
        return jnp.concatenate(parts, axis=0)

    for h in range(heads):
        at = slice(h * HEAD, (h + 1) * HEAD)
        keys = [load(0, g, at) for g in range(blocks)]
        values = [jnp.concatenate([load(1, g, at), ones], axis=1) for g in range(blocks)]
        for first in range(0, blocks, 2):
            pair = [queries[b][mine if b < 2 else slice(None), at] for b in (first, first + 1)]
            q = jnp.concatenate(pair, axis=0)
            peak = summed = None
            for s in range(blocks):
                sc = nt(q, keys[s])
                if s // 2 == first // 2:
                    halves = [sc[:rows], sc[rows:]]
                    own = [halves[s % 2][:, j * rows : (j + 1) * rows] for j in range(4)]
                    own[part] = jnp.full((rows, rows), -1e30, F32)
                    halves[s % 2] = jnp.concatenate(own, axis=1)
                    sc = jnp.concatenate(halves, axis=0)
                top = jnp.max(sc, axis=-1, keepdims=True)
                top = top if s == 0 else jnp.maximum(peak, top)
                term = nn(jnp.exp2((sc - top) * SCALE2).astype(BF), values[s])
                summed = term if s == 0 else summed * jnp.exp2((peak - top) * SCALE2) + term
                peak = top
            total = summed[:, HEAD:]
            result = (summed[:, :HEAD] / total).astype(BF)
            level_all = peak * SCALE2 + jnp.log2(total)
            for i, b in enumerate((first, first + 1)):
                here = slice(i * rows, (i + 1) * rows)
                outs[b][h * rows : (h + 1) * rows, :] = result[here]
                level = jnp.transpose(level_all[here])[0:EXTRA, :]
                high = level.astype(BF).astype(F32)
                mid = (level - high).astype(BF).astype(F32)
                row = lax.broadcasted_iota(jnp.int32, (EXTRA, HEAD), 0) - 3 * h
                three = jnp.where(row == 0, high, jnp.where(row == 1, mid, level - high - mid))
                levels[b] = three if h == 0 else jnp.where(row < 0, levels[b], three)
    for b in range(blocks):
        outs[b][heads * rows :, :] = levels[b].astype(BF)


def attend_groups(part, pos, queries, cached):
    blocks = len(queries)
    rows, width = queries[-1].shape
    flat = [a for g in cached for a in g]
    arrays = [a for block, _ in flat for a in block]
    places = [(len(block), place) for block, place in flat]
    return pl.pallas_call(
        functools.partial(group_kernel, part, blocks, places),
        in_specs=[SCALARS] + [RESIDENT] * (blocks + len(arrays)),
        out_specs=[RESIDENT] * blocks,
        out_shape=[out_of((rows * width // HEAD + EXTRA, HEAD))] * blocks,
        compiler_params=params(32),
        cost_estimate=SMALL,
        name="attend_groups",
    )(pos, *queries, *arrays)


def out_kernel(part, groups, pos, *refs):
    back = refs[:groups]
    acc, top, total, weight, send, attended = refs[groups:]
    rows = send.shape[0]
    width = acc.shape[1] // groups
    mine = slice(part * rows, (part + 1) * rows)
    for s, block in zip(ORDER[part], back):
        for h in range(width // HEAD):
            cols = pl.ds(pl.multiple_of((pos[0] ^ s) * width + h * HEAD, HEAD), HEAD)
            three = block[rows * width // HEAD :, :].astype(F32)[3 * h : 3 * h + 3, :]
            level = three[0:1, :] + three[1:2, :] + three[2:3, :]
            level = jnp.transpose(jnp.broadcast_to(level, (rows, HEAD)))
            own = top[mine, cols]
            peak = jnp.maximum(level, own)
            w_own, w_back = jnp.exp2(own - peak), jnp.exp2(level - peak)
            mixed = acc[mine, cols] * w_own + block[h * rows : (h + 1) * rows, :].astype(F32) * w_back
            attended[:, cols] = (mixed / (total[mine, cols] * w_own + w_back)).astype(BF)
    project(attended, weight, 1 - pos[1], send)


def project(attended, weight, place, out):
    half = out.shape[1]
    block = math.gcd(half, 768)
    for i in range(0, half, block):
        cols = pl.ds(pl.multiple_of(place * half + i, HEAD), block)
        out[:, i : i + block] = nn(attended[...], weight[:, cols]).astype(out.dtype)


def project_out(part, pos, back, acc, top, total, weight):
    groups = len(back)
    rows, width_all = acc.shape[0] // 2, acc.shape[1]
    return pl.pallas_call(
        functools.partial(out_kernel, part, groups),
        in_specs=[SCALARS] + [RESIDENT] * (groups + 4),
        out_specs=[RESIDENT] * 2,
        out_shape=[out_of((rows, weight.shape[1] // 2)), out_of((rows, width_all))],
        compiler_params=params(32),
        cost_estimate=LARGE,
        name="merge_and_project",
    )(pos, *back, acc, top, total, weight)


def keep_kernel(pos, attended, weight, keep):
    project(attended, weight, pos[1], keep)


def project_kept(pos, attended, weight):
    return pl.pallas_call(
        keep_kernel,
        in_specs=[SCALARS] + [RESIDENT] * 2,
        out_specs=RESIDENT,
        out_shape=out_of((attended.shape[0], weight.shape[1] // 2), F32),
        compiler_params=params(32),
        cost_estimate=SMALL,
        name="project_kept",
    )(pos, attended, weight)


def gated(pos, rows_in, mod, keep, got):
    half = keep.shape[1]
    gate = mod[2, pl.ds(pos[2], 1), pl.ds(pl.multiple_of(pos[1] * half, HEAD), half)]
    return (rows_in.astype(F32) + gate * (keep[...] + got[...].astype(F32))).astype(BF)


def other_rows_kernel(pos, hidden, mod, keep, got, out):
    half = keep.shape[1]
    cols = pl.ds(pl.multiple_of(pos[1] * half, HEAD), half)
    out[...] = gated(pos, hidden[:, cols], mod, keep, got)


def my_rows_kernel(pos, hidden, mod, keep, got, theirs, out, rows, sems):
    half = keep.shape[1]
    mine, other = pos[2], 1 - pos[2]
    copies = [pltpu.make_async_copy(theirs, out.at[other], sems.at[0])]
    copies[0].start()
    block = half // 2
    for i in range(2):
        here = slice(i * block, (i + 1) * block)
        cols = pl.ds(pl.multiple_of(pos[1] * half + i * block, HEAD), block)
        gate = mod[2, pl.ds(mine, 1), cols]
        total = keep[:, here] + got[:, here].astype(F32)
        before = hidden[pl.ds(mine, 1), :, cols][0].astype(F32)
        rows[:, here] = (before + gate * total).astype(BF)
        copy = pltpu.make_async_copy(rows.at[:, here], out.at[mine, :, here], sems.at[i + 1])
        copy.start()
        copies.append(copy)
    for copy in copies:
        copy.wait()


def finish(pos, hidden, mod, keep, got, *theirs):
    scratch = [pltpu.VMEM(keep.shape, BF), pltpu.SemaphoreType.DMA((3,))]
    return pl.pallas_call(
        my_rows_kernel if theirs else other_rows_kernel,
        in_specs=[SCALARS] + [RESIDENT] * (4 + len(theirs)),
        out_specs=ANYWHERE if theirs else RESIDENT,
        out_shape=out_of((2,) * len(theirs) + keep.shape),
        scratch_shapes=scratch if theirs else [],
        compiler_params=params(24),
        cost_estimate=SMALL,
        name="gate_and_add",
    )(pos, hidden, mod, keep, got, *theirs)


def tie(value, *others):
    return lax.optimization_barrier((value, others))[0]


def spread_heads(groups, hidden_states, modulation, qkv_weight, out_weight, qk_gain, stale_kv):
    patches = lax.axis_size("patch")
    inner = patches // groups
    patch = lax.axis_index("patch")
    pos = jnp.stack([patch // inner, lax.axis_index("tp"), patch % 2]).astype(jnp.int32)

    def across(value, bit):
        return lax.ppermute(value, "patch", [(i, i ^ bit) for i in range(patches)])

    def along(value, step):
        return across(value, inner * step)

    weights = jnp.transpose(qkv_weight, (1, 0, 2))
    step = lax.optimization_barrier

    cut = cut_stale(pos, stale_kv, groups)
    near, two, one = cut[:1], [along(cut[2], 2)], [along(cut[1], 1)]
    far_near = [across(near[0], 2)]
    hidden_now = tie(hidden_states, *cut)
    hidden_for = lax.dynamic_index_in_dim(hidden_now, 1 - pos[2], 0, keepdims=False)
    hidden_got = across(hidden_for, 1)
    normed, queries, *slots = make_queries(
        pos, hidden_states, hidden_got, modulation, qk_gain, weights, groups
    )
    normed, queries, slots, near, one, far_near, cut_three = step(
        (normed, queries, slots, near, one, far_near, cut[3])
    )

    three = [along(cut_three, 3)]
    far_one = [across(a, 2) for a in halves(one[0])]
    fresh = make_fresh(0, normed, qk_gain, weights)
    two, far_one, fresh, slots, queries, normed = step(
        (two, far_one, fresh, slots, queries, normed)
    )

    parts = halves(two[0])
    far_two = [across(a, 2) for a in parts]
    asked = [slots[0], along(tie(slots[1], *parts), 1)]
    swap_a = [across(pack(pos, near, far_near, one, far_one), 1)]
    fresh = make_fresh(1, normed, qk_gain, weights, fresh)
    three, far_two, asked, fresh, slots, queries = step(
        (three, far_two, asked, fresh, slots, queries)
    )

    far_three = [across(three[0], 2)]
    their_far = [along(slots[2 * s - 1], s) for s in (2, 3)]
    swap_b = [across(pack(pos, two, far_two, three), 1)]
    own = attend_own(queries, *fresh)
    far_three, their_far, asked, swap_a, swap_b, own, slots = step(
        (far_three, their_far, asked, swap_a, swap_b, own, slots)
    )

    my_far = [along(slots[2 * s - 2], s) for s in (2, 3)]
    their_queries, my_queries = asked + their_far, asked + my_far
    held = [
        [(near, None), (swap_a, 0), (far_near, None), (swap_a, 1)],
        [(one, None), (swap_a, 2), (far_one, None), (swap_a, 3)],
        [(two, None), (swap_b, 0), (far_two, None), (swap_b, 1)],
        [(three, None), (swap_b, 2), (far_three, None), ([across(far_three[0], 1)], None)],
    ]
    theirs = attend_groups(1, pos, their_queries, held)
    theirs, my_queries = step((theirs, my_queries))
    back = [theirs[0]] + [along(a, s) for a, s in zip(theirs[1:], ORDER[1][1:])]
    my_queries[0] = tie(my_queries[0], theirs)
    mine = attend_groups(0, pos, my_queries, held)
    mine_back = [mine[0]] + [along(a, s) for a, s in zip(mine[1:], ORDER[0][1:])]
    back[0] = tie(back[0], mine)
    swap = [(0, 1), (1, 0)]
    send, attended = project_out(1, pos, back, *own, out_weight)
    got = lax.ppermute(send, "tp", swap)
    mine_back[0] = tie(mine_back[0], send)

    my_send, my_attended = project_out(0, pos, mine_back, *own, out_weight)
    my_got = lax.ppermute(my_send, "tp", swap)
    fresh_got = across(tie(fresh[1], send), 1)
    fresh_kv = place_fresh(pos, tie(fresh[0], my_send), fresh_got)
    keep = project_kept(pos, tie(attended, my_send), out_weight)
    my_keep = project_kept(pos, my_attended, out_weight)
    theirs = finish(pos, hidden_got, modulation, keep, got)
    mixed = finish(pos, hidden_states, modulation, my_keep, my_got, across(theirs, 1))
    return mixed, fresh_kv


def head_norm(values_in, gain_row, heads_here):
    shaped = values_in.reshape(values_in.shape[0], values_in.shape[1], heads_here, HEAD)
    square_mean = jnp.mean(shaped * shaped, axis=-1, keepdims=True)
    return (shaped * lax.rsqrt(square_mean + 1e-06) * gain_row).astype(BF)


def gather_all(hidden_states, modulation, qkv_weight, out_weight, qk_gain, stale_kv):
    clip_count, row_count, width_all = hidden_states.shape
    heads_here = qkv_weight.shape[2] // HEAD
    inputs = hidden_states.astype(F32)
    feature_mean = jnp.mean(inputs, axis=-1, keepdims=True)
    centered = inputs - feature_mean
    feature_var = jnp.mean(centered * centered, axis=-1, keepdims=True)
    normed = (
        centered * lax.rsqrt(feature_var + 1e-06) * (1.0 + modulation[1][:, None, :])
        + modulation[0][:, None, :]
    ).astype(BF)
    projected = jnp.einsum("ctd,dkh->kcth", normed, qkv_weight, preferred_element_type=F32)
    queries = head_norm(projected[0], qk_gain[0], heads_here)
    keys_new = head_norm(projected[1], qk_gain[1], heads_here)
    values_new = projected[2].astype(BF).reshape(clip_count, row_count, heads_here, HEAD)
    fresh_kv = jnp.stack(
        [keys_new.reshape(clip_count, row_count, -1), values_new.reshape(clip_count, row_count, -1)]
    )
    own_first = lax.axis_index("patch") * row_count
    gathered = lax.all_gather(stale_kv, "patch", axis=2, tiled=True)
    gathered = lax.dynamic_update_slice_in_dim(gathered, fresh_kv, own_first, 2)
    count = gathered.shape[2]
    tile_keys = gathered[0].reshape(clip_count, count, heads_here, HEAD)
    tile_values = gathered[1].reshape(clip_count, count, heads_here, HEAD)
    scores = jnp.einsum("cqhd,ckhd->chqk", queries, tile_keys, preferred_element_type=F32)
    scores = scores * HEAD ** (-0.5)
    expo = jnp.exp(scores - jnp.max(scores, axis=-1, keepdims=True))
    summed = jnp.einsum(
        "chqk,ckhd->chqd", expo.astype(BF), tile_values, preferred_element_type=F32
    )
    attended = (summed / jnp.sum(expo, axis=-1)[..., None]).astype(BF)
    attended = jnp.transpose(attended, (0, 2, 1, 3)).reshape(clip_count, row_count, -1)
    product = jnp.einsum("cth,hd->ctd", attended, out_weight, preferred_element_type=F32)
    col_count = width_all // lax.axis_size("tp")
    col_first = lax.axis_index("tp") * col_count
    summed_part = lax.psum_scatter(
        product.astype(BF), "tp", scatter_dimension=2, tiled=True
    ).astype(F32)
    input_part = lax.dynamic_slice_in_dim(inputs, col_first, col_count, 2)
    gate_part = lax.dynamic_slice_in_dim(modulation[2], col_first, col_count, 1)
    mixed = (input_part + gate_part[:, None, :] * summed_part).astype(BF)
    return (mixed, fresh_kv)


def per_device(*arrays):
    clips = arrays[0].shape[0]
    heads_here = arrays[2].shape[2] // HEAD
    patches = lax.axis_size("patch")
    groups = math.gcd(heads_here, patches)
    if clips == 2 and groups == 4 and heads_here <= 5 * groups and patches == 4 * groups and lax.axis_size("tp") == 2:
        return spread_heads(groups, *arrays)
    return gather_all(*arrays)


def solution(mesh):
    in_specs = (
        P(None, "patch", None),
        P(),
        P(None, None, "tp"),
        P("tp", None),
        P(),
        P(None, None, "patch", "tp"),
    )
    out_specs = (P(None, "patch", "tp"), P(None, None, "patch", "tp"))
    return jax.shard_map(
        per_device, mesh=mesh, in_specs=in_specs, out_specs=out_specs, check_vma=False
    )
```

```python
import functools
import math

import jax
import jax.numpy as jnp
from jax import lax
from jax.experimental import pallas as pl
from jax.experimental.pallas import tpu as pltpu
from jax.sharding import PartitionSpec as P

HEAD = 128
EXTRA = 16
LOG2E = 1.4426950408889634
SCALE2 = HEAD ** (-0.5) * LOG2E
ORDER = ((0, 1, 3, 2), (0, 3, 2, 1))
MIB = 1024 * 1024
BF = jnp.bfloat16
F32 = jnp.float32


SMALL = pl.CostEstimate(flops=1000, bytes_accessed=1000, transcendentals=0)
LARGE = pl.CostEstimate(flops=10**10, bytes_accessed=10**8, transcendentals=0)


def nt(a, b):
    return lax.dot_general(a, b, (((1,), (1,)), ((), ())), preferred_element_type=F32)


def nn(a, b):
    return lax.dot_general(a, b, (((1,), (0,)), ((), ())), preferred_element_type=F32)


def params(mib, **kw):
    return pltpu.CompilerParams(vmem_limit_bytes=mib * MIB, **kw)


def norm_heads(values, gain_row):
    parts = []
    for h in range(values.shape[1] // HEAD):
        v = values[:, h * HEAD : (h + 1) * HEAD]
        square_mean = jnp.mean(v * v, axis=-1, keepdims=True)
        parts.append((v * lax.rsqrt(square_mean + 1e-06) * gain_row).astype(BF))
    return jnp.concatenate(parts, axis=1)


def full(shape):
    return pl.BlockSpec(shape, lambda *_: (0,) * len(shape))


def out_of(shape, dtype=BF):
    return jax.ShapeDtypeStruct(shape, dtype)


ANYWHERE = pl.BlockSpec(memory_space=pltpu.HBM)
SCALARS = pl.BlockSpec(memory_space=pltpu.SMEM)
RESIDENT = pl.BlockSpec(memory_space=pltpu.VMEM)


def copy_all(sems, pairs):
    copies = [pltpu.make_async_copy(a, b, sems.at[i]) for i, (a, b) in enumerate(pairs)]
    for c in copies:
        c.start()
    for c in copies:
        c.wait()


def cut_kernel(width, pos, stale, *refs):
    outs, held, sems = refs[:-2], refs[-2], refs[-1]
    slabs = [(kv, c) for kv in range(held.shape[0]) for c in range(held.shape[1])]
    copies = [
        pltpu.make_async_copy(stale.at[kv, c], held.at[kv, c], sems.at[i])
        for i, (kv, c) in enumerate(slabs)
    ]
    for copy in copies:
        copy.start()
    for (kv, c), copy in zip(slabs, copies):
        copy.wait()
        for s, out in enumerate(outs):
            out[kv, c] = held[kv, c, :, pl.ds(pl.multiple_of((pos[0] ^ s) * width, HEAD), width)]


def cut_stale(pos, stale, groups):
    kv, clips, rows, cols = stale.shape
    width = cols // groups
    return pl.pallas_call(
        functools.partial(cut_kernel, width),
        out_shape=[out_of((kv, clips, rows, width))] * groups,
        in_specs=[SCALARS, ANYWHERE],
        out_specs=[RESIDENT] * groups,
        scratch_shapes=[pltpu.VMEM(stale.shape, BF), pltpu.SemaphoreType.DMA((kv * clips,))],
        compiler_params=params(8),
        name="cut_stale",
    )(pos, pltpu.with_memory_space_constraint(stale, pltpu.HBM))


def halves_kernel(block, keys, values):
    keys[...] = block[0]
    values[...] = block[1]


def halves(block):
    return pl.pallas_call(
        halves_kernel,
        out_shape=[out_of(block.shape[1:])] * 2,
        in_specs=[RESIDENT],
        out_specs=[RESIDENT] * 2,
        compiler_params=params(8),
        name="halves",
    )(block)


def pack_kernel(counts, pos, *refs):
    refs, out = list(refs[:-1]), refs[-1]
    other = pl.ds(1 - pos[2], 1)
    for i, count in enumerate(counts):
        if count == 1:
            out[i] = refs.pop(0)[:, other][:, 0]
        else:
            for kv in range(2):
                out[i, kv] = refs.pop(0)[other][0]


def pack(pos, *blocks):
    rows, width = blocks[0][0].shape[-2:]
    flat = [a for block in blocks for a in block]
    return pl.pallas_call(
        functools.partial(pack_kernel, [len(block) for block in blocks]),
        out_shape=out_of((len(blocks), 2, rows, width)),
        in_specs=[SCALARS] + [RESIDENT] * len(flat),
        out_specs=RESIDENT,
        compiler_params=params(8),
        name="pack",
    )(pos, *flat)


def query_kernel(groups, per_step, pos, hidden, got, mod, gain, weight, normed, whole, *slots):
    rows = got.shape[0]
    step = pl.program_id(0)

    @pl.when(step == 0)
    def _():
        chunk = 32
        shift, scale = mod[0, pl.ds(pos[2], 1), :], 1.0 + mod[1, pl.ds(pos[2], 1), :]
        for half in range(2):
            for r in range(0, rows, chunk):
                x = hidden[0, r : r + chunk, :] if half == 0 else got[r : r + chunk, :]
                x = x.astype(F32)
                centered = x - jnp.mean(x, axis=-1, keepdims=True)
                var = jnp.mean(centered * centered, axis=-1, keepdims=True)
                y = centered * lax.rsqrt(var + 1e-06) * scale + shift
                normed[half * rows + r : half * rows + r + chunk, :] = y.astype(BF)

    q = norm_heads(nn(normed[...], weight[0]), gain[0:1, :])
    whole[...] = q
    width = q.shape[1] // per_step
    for j in range(per_step):
        part = q[:, j * width : (j + 1) * width]
        slot = (step * per_step + j) ^ pos[0]
        for s in range(groups):

            @pl.when(slot == s)
            def _(s=s, part=part):
                if s < 2:
                    slots[s][...] = part
                else:
                    slots[2 * s - 2][...] = part[:rows]
                    slots[2 * s - 1][...] = part[rows:]


def make_queries(pos, hidden, got, mod, gain, weight, groups):
    rows, width_all = got.shape
    cols = weight.shape[2]
    per_step = 2 if groups % 2 == 0 else 1
    steps = groups // per_step
    width = cols // groups
    wide = width * per_step
    return pl.pallas_call(
        functools.partial(query_kernel, groups, per_step),
        grid_spec=pltpu.PrefetchScalarGridSpec(
            num_scalar_prefetch=1,
            grid=(steps,),
            in_specs=[
                pl.BlockSpec((1, rows, width_all), lambda i, pos: (pos[2], 0, 0)),
                full(got.shape),
                full(mod.shape),
                full(gain.shape),
                pl.BlockSpec((1, width_all, wide), lambda i, pos: (0, 0, i)),
            ],
            out_specs=[
                full((2 * rows, width_all)),
                pl.BlockSpec((2 * rows, wide), lambda i, pos: (0, i)),
            ]
            + [full((2 * rows, width))] * 2
            + [full((rows, width))] * (2 * groups - 4),
        ),
        out_shape=[out_of((2 * rows, width_all)), out_of((2 * rows, cols))]
        + [out_of((2 * rows, width))] * 2
        + [out_of((rows, width))] * (2 * groups - 4),
        compiler_params=params(32),
        cost_estimate=SMALL,
        name="norm_and_queries",
    )(pos, hidden, got, mod, gain, weight)


def fresh_kernel(slot, normed, gain, weight, *refs):
    mine, other = refs[-2:]
    rows = mine.shape[1]
    made = nn(normed[...], weight[0])
    made = norm_heads(made, gain[1:2, :]) if slot == 0 else made.astype(BF)
    mine[0] = made[:rows]
    other[0] = made[rows:]


def make_fresh(slot, normed, gain, weight, before=()):
    rows, width_all = normed.shape
    cols = weight.shape[2]
    block = math.gcd(cols, 768)
    out = pl.BlockSpec((1, rows // 2, block), lambda i: (slot, 0, i))
    return pl.pallas_call(
        functools.partial(fresh_kernel, slot),
        grid=(cols // block,),
        in_specs=[
            full(normed.shape),
            full(gain.shape),
            pl.BlockSpec((1, width_all, block), lambda i: (slot + 1, 0, i)),
        ]
        + [ANYWHERE] * len(before),
        out_specs=[out, out],
        out_shape=[out_of((2, rows // 2, cols))] * 2,
        input_output_aliases={3 + i: i for i in range(len(before))},
        compiler_params=params(32),
        cost_estimate=SMALL,
        name="fresh_keys" if slot == 0 else "fresh_values",
    )(normed, gain, weight, *before)


def place_kernel(pos, mine, got, out, sems):
    clip = pos[2]
    copy_all(sems, [(mine, out.at[:, clip]), (got, out.at[:, 1 - clip])])


def place_fresh(pos, mine, got):
    kv, rows, cols = mine.shape
    return pl.pallas_call(
        place_kernel,
        out_shape=out_of((kv, 2, rows, cols)),
        in_specs=[SCALARS, ANYWHERE, ANYWHERE],
        out_specs=ANYWHERE,
        scratch_shapes=[pltpu.SemaphoreType.DMA((2,))],
        compiler_params=params(8),
        name="place_fresh",
    )(pos, mine, got)


def own_kernel(q, mine, other, acc, top, total):
    rows = mine.shape[1]
    ones = jnp.ones((rows, HEAD), BF)
    heads = q.shape[1] // HEAD
    for j, kv in enumerate((mine, other)):
        here = slice(j * rows, (j + 1) * rows)
        for first in range(0, heads, 3):
            ats = [slice(h * HEAD, (h + 1) * HEAD) for h in range(first, min(first + 3, heads))]
            scores = [nt(q[here, at], kv[0, :, at]) for at in ats]
            values = [jnp.concatenate([kv[1, :, at], ones], axis=1) for at in ats]
            peaks = [jnp.max(sc, axis=-1, keepdims=True) for sc in scores]
            weights = [jnp.exp2((sc - p) * SCALE2).astype(BF) for sc, p in zip(scores, peaks)]
            summed = [nn(w, v) for w, v in zip(weights, values)]
            for at, p, s in zip(ats, peaks, summed):
                acc[here, at] = s[:, :HEAD]
                total[here, at] = s[:, HEAD:]
                top[here, at] = jnp.broadcast_to(p * SCALE2, (rows, HEAD))


def attend_own(queries, mine, other):
    block = math.gcd(queries.shape[1], 768)
    rows, cols = queries.shape
    wide = pl.BlockSpec((rows, block), lambda i: (0, i))
    kv = pl.BlockSpec((2, rows // 2, block), lambda i: (0, 0, i))
    return pl.pallas_call(
        own_kernel,
        grid=(cols // block,),
        in_specs=[wide, kv, kv],
        out_specs=[wide] * 3,
        out_shape=[out_of((rows, cols), F32)] * 3,
        compiler_params=params(24),
        cost_estimate=SMALL,
        name="attend_own",
    )(queries, mine, other)


def group_kernel(part, blocks, places, pos, *refs):
    count = sum(n for n, _ in places)
    queries, refs, outs = refs[:blocks], list(refs[blocks : blocks + count]), refs[blocks + count :]
    outs = [outs[ORDER[part].index(b)] for b in range(blocks)]
    cached = [[refs.pop(0) for _ in range(n)] for n, _ in places]
    rows, width = queries[-1].shape
    mine = slice(part * rows, (part + 1) * rows)
    clip = pl.ds(pos[2], 1)
    ones = jnp.ones((4 * rows, HEAD), BF)
    heads, levels = width // HEAD, [None] * blocks

    def load(kv, group, at):
        parts = []
        for block, (n, place) in list(zip(cached, places))[4 * group : 4 * group + 4]:
            if place is not None:
                parts.append(block[0][place, kv, :, at])
            elif n == 2:
                parts.append(block[kv][clip, :, at][0])
            else:
                parts.append(block[0][kv, clip, :, at][0])
        return jnp.concatenate(parts, axis=0)

    for h in range(heads):
        at = slice(h * HEAD, (h + 1) * HEAD)
        keys = [load(0, g, at) for g in range(blocks)]
        values = [jnp.concatenate([load(1, g, at), ones], axis=1) for g in range(blocks)]
        for first in range(0, blocks, 2):
            pair = [queries[b][mine if b < 2 else slice(None), at] for b in (first, first + 1)]
            q = jnp.concatenate(pair, axis=0)
            peak = summed = None
            for s in range(blocks):
                sc = nt(q, keys[s])
                if s // 2 == first // 2:
                    halves = [sc[:rows], sc[rows:]]
                    own = [halves[s % 2][:, j * rows : (j + 1) * rows] for j in range(4)]
                    own[part] = jnp.full((rows, rows), -1e30, F32)
                    halves[s % 2] = jnp.concatenate(own, axis=1)
                    sc = jnp.concatenate(halves, axis=0)
                top = jnp.max(sc, axis=-1, keepdims=True)
                top = top if s == 0 else jnp.maximum(peak, top)
                term = nn(jnp.exp2((sc - top) * SCALE2).astype(BF), values[s])
                summed = term if s == 0 else summed * jnp.exp2((peak - top) * SCALE2) + term
                peak = top
            total = summed[:, HEAD:]
            result = (summed[:, :HEAD] / total).astype(BF)
            level_all = peak * SCALE2 + jnp.log2(total)
            for i, b in enumerate((first, first + 1)):
                here = slice(i * rows, (i + 1) * rows)
                outs[b][h * rows : (h + 1) * rows, :] = result[here]
                level = jnp.transpose(level_all[here])[0:EXTRA, :]
                high = level.astype(BF).astype(F32)
                mid = (level - high).astype(BF).astype(F32)
                row = lax.broadcasted_iota(jnp.int32, (EXTRA, HEAD), 0) - 3 * h
                three = jnp.where(row == 0, high, jnp.where(row == 1, mid, level - high - mid))
                levels[b] = three if h == 0 else jnp.where(row < 0, levels[b], three)
    for b in range(blocks):
        outs[b][heads * rows :, :] = levels[b].astype(BF)


def attend_groups(part, pos, queries, cached):
    blocks = len(queries)
    rows, width = queries[-1].shape
    flat = [a for g in cached for a in g]
    arrays = [a for block, _ in flat for a in block]
    places = [(len(block), place) for block, place in flat]
    return pl.pallas_call(
        functools.partial(group_kernel, part, blocks, places),
        in_specs=[SCALARS] + [RESIDENT] * (blocks + len(arrays)),
        out_specs=[RESIDENT] * blocks,
        out_shape=[out_of((rows * width // HEAD + EXTRA, HEAD))] * blocks,
        compiler_params=params(32),
        cost_estimate=SMALL,
        name="attend_groups",
    )(pos, *queries, *arrays)


def out_kernel(part, groups, pos, *refs):
    back = refs[:groups]
    acc, top, total, weight, send, attended = refs[groups:]
    rows = send.shape[0]
    width = acc.shape[1] // groups
    mine = slice(part * rows, (part + 1) * rows)
    for s, block in zip(ORDER[part], back):
        for h in range(width // HEAD):
            cols = pl.ds(pl.multiple_of((pos[0] ^ s) * width + h * HEAD, HEAD), HEAD)
            three = block[rows * width // HEAD :, :].astype(F32)[3 * h : 3 * h + 3, :]
            level = three[0:1, :] + three[1:2, :] + three[2:3, :]
            level = jnp.transpose(jnp.broadcast_to(level, (rows, HEAD)))
            own = top[mine, cols]
            peak = jnp.maximum(level, own)
            w_own, w_back = jnp.exp2(own - peak), jnp.exp2(level - peak)
            mixed = acc[mine, cols] * w_own + block[h * rows : (h + 1) * rows, :].astype(F32) * w_back
            attended[:, cols] = (mixed / (total[mine, cols] * w_own + w_back)).astype(BF)
    project(attended, weight, 1 - pos[1], send)


def project(attended, weight, place, out):
    half = out.shape[1]
    block = math.gcd(half, 768)
    for i in range(0, half, block):
        cols = pl.ds(pl.multiple_of(place * half + i, HEAD), block)
        out[:, i : i + block] = nn(attended[...], weight[:, cols]).astype(out.dtype)


def project_out(part, pos, back, acc, top, total, weight):
    groups = len(back)
    rows, width_all = acc.shape[0] // 2, acc.shape[1]
    return pl.pallas_call(
        functools.partial(out_kernel, part, groups),
        in_specs=[SCALARS] + [RESIDENT] * (groups + 4),
        out_specs=[RESIDENT] * 2,
        out_shape=[out_of((rows, weight.shape[1] // 2)), out_of((rows, width_all))],
        compiler_params=params(32),
        cost_estimate=LARGE,
        name="merge_and_project",
    )(pos, *back, acc, top, total, weight)


def keep_kernel(pos, attended, weight, keep):
    project(attended, weight, pos[1], keep)


def project_kept(pos, attended, weight):
    return pl.pallas_call(
        keep_kernel,
        in_specs=[SCALARS] + [RESIDENT] * 2,
        out_specs=RESIDENT,
        out_shape=out_of((attended.shape[0], weight.shape[1] // 2), F32),
        compiler_params=params(32),
        cost_estimate=SMALL,
        name="project_kept",
    )(pos, attended, weight)


def gated(pos, rows_in, mod, keep, got):
    half = keep.shape[1]
    gate = mod[2, pl.ds(pos[2], 1), pl.ds(pl.multiple_of(pos[1] * half, HEAD), half)]
    return (rows_in.astype(F32) + gate * (keep[...] + got[...].astype(F32))).astype(BF)


def other_rows_kernel(pos, hidden, mod, keep, got, out):
    half = keep.shape[1]
    cols = pl.ds(pl.multiple_of(pos[1] * half, HEAD), half)
    out[...] = gated(pos, hidden[:, cols], mod, keep, got)


def my_rows_kernel(pos, hidden, mod, keep, got, theirs, out, rows, sems):
    half = keep.shape[1]
    mine, other = pos[2], 1 - pos[2]
    copies = [pltpu.make_async_copy(theirs, out.at[other], sems.at[0])]
    copies[0].start()
    block = half // 2
    for i in range(2):
        here = slice(i * block, (i + 1) * block)
        cols = pl.ds(pl.multiple_of(pos[1] * half + i * block, HEAD), block)
        gate = mod[2, pl.ds(mine, 1), cols]
        total = keep[:, here] + got[:, here].astype(F32)
        before = hidden[pl.ds(mine, 1), :, cols][0].astype(F32)
        rows[:, here] = (before + gate * total).astype(BF)
        copy = pltpu.make_async_copy(rows.at[:, here], out.at[mine, :, here], sems.at[i + 1])
        copy.start()
        copies.append(copy)
    for copy in copies:
        copy.wait()


def finish(pos, hidden, mod, keep, got, *theirs):
    scratch = [pltpu.VMEM(keep.shape, BF), pltpu.SemaphoreType.DMA((3,))]
    return pl.pallas_call(
        my_rows_kernel if theirs else other_rows_kernel,
        in_specs=[SCALARS] + [RESIDENT] * (4 + len(theirs)),
        out_specs=ANYWHERE if theirs else RESIDENT,
        out_shape=out_of((2,) * len(theirs) + keep.shape),
        scratch_shapes=scratch if theirs else [],
        compiler_params=params(24),
        cost_estimate=SMALL,
        name="gate_and_add",
    )(pos, hidden, mod, keep, got, *theirs)


def tie(value, *others):
    return lax.optimization_barrier((value, others))[0]


def spread_heads(groups, hidden_states, modulation, qkv_weight, out_weight, qk_gain, stale_kv):
    patches = lax.axis_size("patch")
    inner = patches // groups
    patch = lax.axis_index("patch")
    pos = jnp.stack([patch // inner, lax.axis_index("tp"), patch % 2]).astype(jnp.int32)

    def across(value, bit):
        return lax.ppermute(value, "patch", [(i, i ^ bit) for i in range(patches)])

    def along(value, step):
        return across(value, inner * step)

    weights = jnp.transpose(qkv_weight, (1, 0, 2))
    step = lax.optimization_barrier

    cut = cut_stale(pos, stale_kv, groups)
    near, two, one = cut[:1], [along(cut[2], 2)], [along(cut[1], 1)]
    far_near = [across(near[0], 2)]
    hidden_now = tie(hidden_states, *cut)
    hidden_for = lax.dynamic_index_in_dim(hidden_now, 1 - pos[2], 0, keepdims=False)
    hidden_got = across(hidden_for, 1)
    in_place = pltpu.with_memory_space_constraint(hidden_states, pltpu.HBM)
    normed, queries, *slots = make_queries(
        pos, in_place, hidden_got, modulation, qk_gain, weights, groups
    )
    normed, queries, slots, near, one, far_near, cut_three = step(
        (normed, queries, slots, near, one, far_near, cut[3])
    )

    three = [along(cut_three, 3)]
    far_one = [across(a, 2) for a in halves(one[0])]
    fresh = make_fresh(0, normed, qk_gain, weights)
    two, far_one, fresh, slots, queries, normed = step(
        (two, far_one, fresh, slots, queries, normed)
    )

    parts = halves(two[0])
    far_two = [across(a, 2) for a in parts]
    asked = [slots[0], along(tie(slots[1], *parts), 1)]
    swap_a = [across(pack(pos, near, far_near, one, far_one), 1)]
    fresh = make_fresh(1, normed, qk_gain, weights, fresh)
    three, far_two, asked, fresh, slots, queries = step(
        (three, far_two, asked, fresh, slots, queries)
    )

    far_three = [across(three[0], 2)]
    their_far = [along(slots[2 * s - 1], s) for s in (2, 3)]
    swap_b = [across(pack(pos, two, far_two, three), 1)]
    own = attend_own(queries, *fresh)
    far_three, their_far, asked, swap_a, swap_b, own, slots = step(
        (far_three, their_far, asked, swap_a, swap_b, own, slots)
    )

    my_far = [along(slots[2 * s - 2], s) for s in (2, 3)]
    their_queries, my_queries = asked + their_far, asked + my_far
    held = [
        [(near, None), (swap_a, 0), (far_near, None), (swap_a, 1)],
        [(one, None), (swap_a, 2), (far_one, None), (swap_a, 3)],
        [(two, None), (swap_b, 0), (far_two, None), (swap_b, 1)],
        [(three, None), (swap_b, 2), (far_three, None), ([across(far_three[0], 1)], None)],
    ]
    theirs = attend_groups(1, pos, their_queries, held)
    theirs, my_queries = step((theirs, my_queries))
    back = [theirs[0]] + [along(a, s) for a, s in zip(theirs[1:], ORDER[1][1:])]
    my_queries[0] = tie(my_queries[0], theirs)
    mine = attend_groups(0, pos, my_queries, held)
    mine_back = [mine[0]] + [along(a, s) for a, s in zip(mine[1:], ORDER[0][1:])]
    back[0] = tie(back[0], mine)
    swap = [(0, 1), (1, 0)]
    send, attended = project_out(1, pos, back, *own, out_weight)
    got = lax.ppermute(send, "tp", swap)
    mine_back[0] = tie(mine_back[0], send)

    my_send, my_attended = project_out(0, pos, mine_back, *own, out_weight)
    my_got = lax.ppermute(my_send, "tp", swap)
    fresh_got = across(tie(fresh[1], send), 1)
    fresh_kv = place_fresh(pos, tie(fresh[0], my_send), fresh_got)
    keep = project_kept(pos, tie(attended, my_send), out_weight)
    my_keep = project_kept(pos, my_attended, out_weight)
    theirs = finish(pos, hidden_got, modulation, keep, got)
    mixed = finish(pos, hidden_states, modulation, my_keep, my_got, across(theirs, 1))
    return mixed, fresh_kv


def head_norm(values_in, gain_row, heads_here):
    shaped = values_in.reshape(values_in.shape[0], values_in.shape[1], heads_here, HEAD)
    square_mean = jnp.mean(shaped * shaped, axis=-1, keepdims=True)
    return (shaped * lax.rsqrt(square_mean + 1e-06) * gain_row).astype(BF)


def gather_all(hidden_states, modulation, qkv_weight, out_weight, qk_gain, stale_kv):
    clip_count, row_count, width_all = hidden_states.shape
    heads_here = qkv_weight.shape[2] // HEAD
    inputs = hidden_states.astype(F32)
    feature_mean = jnp.mean(inputs, axis=-1, keepdims=True)
    centered = inputs - feature_mean
    feature_var = jnp.mean(centered * centered, axis=-1, keepdims=True)
    normed = (
        centered * lax.rsqrt(feature_var + 1e-06) * (1.0 + modulation[1][:, None, :])
        + modulation[0][:, None, :]
    ).astype(BF)
    projected = jnp.einsum("ctd,dkh->kcth", normed, qkv_weight, preferred_element_type=F32)
    queries = head_norm(projected[0], qk_gain[0], heads_here)
    keys_new = head_norm(projected[1], qk_gain[1], heads_here)
    values_new = projected[2].astype(BF).reshape(clip_count, row_count, heads_here, HEAD)
    fresh_kv = jnp.stack(
        [keys_new.reshape(clip_count, row_count, -1), values_new.reshape(clip_count, row_count, -1)]
    )
    own_first = lax.axis_index("patch") * row_count
    gathered = lax.all_gather(stale_kv, "patch", axis=2, tiled=True)
    gathered = lax.dynamic_update_slice_in_dim(gathered, fresh_kv, own_first, 2)
    count = gathered.shape[2]
    tile_keys = gathered[0].reshape(clip_count, count, heads_here, HEAD)
    tile_values = gathered[1].reshape(clip_count, count, heads_here, HEAD)
    scores = jnp.einsum("cqhd,ckhd->chqk", queries, tile_keys, preferred_element_type=F32)
    scores = scores * HEAD ** (-0.5)
    expo = jnp.exp(scores - jnp.max(scores, axis=-1, keepdims=True))
    summed = jnp.einsum(
        "chqk,ckhd->chqd", expo.astype(BF), tile_values, preferred_element_type=F32
    )
    attended = (summed / jnp.sum(expo, axis=-1)[..., None]).astype(BF)
    attended = jnp.transpose(attended, (0, 2, 1, 3)).reshape(clip_count, row_count, -1)
    product = jnp.einsum("cth,hd->ctd", attended, out_weight, preferred_element_type=F32)
    col_count = width_all // lax.axis_size("tp")
    col_first = lax.axis_index("tp") * col_count
    summed_part = lax.psum_scatter(
        product.astype(BF), "tp", scatter_dimension=2, tiled=True
    ).astype(F32)
    input_part = lax.dynamic_slice_in_dim(inputs, col_first, col_count, 2)
    gate_part = lax.dynamic_slice_in_dim(modulation[2], col_first, col_count, 1)
    mixed = (input_part + gate_part[:, None, :] * summed_part).astype(BF)
    return (mixed, fresh_kv)


def per_device(*arrays):
    clips = arrays[0].shape[0]
    heads_here = arrays[2].shape[2] // HEAD
    patches = lax.axis_size("patch")
    groups = math.gcd(heads_here, patches)
    if clips == 2 and groups == 4 and heads_here <= 5 * groups and patches == 4 * groups and lax.axis_size("tp") == 2:
        return spread_heads(groups, *arrays)
    return gather_all(*arrays)


def solution(mesh):
    in_specs = (
        P(None, "patch", None),
        P(),
        P(None, None, "tp"),
        P("tp", None),
        P(),
        P(None, None, "patch", "tp"),
    )
    out_specs = (P(None, "patch", "tp"), P(None, None, "patch", "tp"))
    return jax.shard_map(
        per_device, mesh=mesh, in_specs=in_specs, out_specs=out_specs, check_vma=False
    )
```
